128 devices in a mesh: seq: 64 (over y_hi, x, z, core), rep: 2 (over y_lo).
Axes of the slice: x: 4, y: 4 (y_hi: 2, y_lo: 2; y = y_hi * 2 + y_lo), z: 4, core: 2. Of those that a mesh axis runs over, the one named last changes fastest.
Arguments:
- tokens: bfloat16 [2, 16384, 768], P('rep', 'seq'), may hold values from -6 to 6
- router: float32 [768], replicated, may hold values from -0.21875 to 0.21875
- gain_one: float32 [768], replicated, may hold values from 0.5 to 1.5
- bias_one: float32 [768], replicated, may hold values from -1.8 to 1.8
- w_query: bfloat16 [768, 768], replicated, may hold values from -0.21875 to 0.21875
- w_key: bfloat16 [768, 768], replicated, may hold values from -0.21875 to 0.21875
- w_value: bfloat16 [768, 768], replicated, may hold values from -0.21875 to 0.21875
- w_out: bfloat16 [768, 768], replicated, may hold values from -0.875 to 0.875
- gain_two: float32 [768], replicated, may hold values from 0.5 to 1.5
- bias_two: float32 [768], replicated, may hold values from -1.8 to 1.8
- w_expand: bfloat16 [768, 3072], replicated, may hold values from -0.21875 to 0.21875
- w_contract: bfloat16 [3072, 768], replicated, may hold values from -0.109375 to 0.109375
- cotangent: bfloat16 [2, 16384, 768], P('rep', 'seq'), may hold values from -6 to 6
- seq_ids: int32 [2, 16384], P('rep', 'seq'), may hold values from 0 to 16384, as said below
- routed_rows: int32 [2, 64, 48], P('rep', 'seq'), may hold values from 0 to 255, as said below
- routed_count: int32 [2, 64], P('rep', 'seq'), may hold values from 16 to 48, as said below
Outputs:
- output: bfloat16 [2, 16384, 768], P('rep', 'seq')
- input_grad: bfloat16 [2, 16384, 768], P('rep', 'seq')
- router_grad: float32 [768], replicated
- gain_one_grad: float32 [768], replicated
- bias_one_grad: float32 [768], replicated
- query_grad: float32 [768, 768], replicated
- key_grad: float32 [768, 768], replicated
- value_grad: float32 [768, 768], replicated
- out_grad: float32 [768, 768], replicated
- gain_two_grad: float32 [768], replicated
- bias_two_grad: float32 [768], replicated
- expand_grad: float32 [768, 3072], replicated
- contract_grad: float32 [3072, 768], replicated
The draws below stay inside these ranges and needn't reach their ends.
Inputs may be any that keep to these rules, and one draw needn't show every extreme that they name: `seq_ids`: sequence 0 of a group is one document cut into contiguous pieces, piece j at the head of device j, 64 to 128 tokens each, so that its token order is the group's order; every other id names a short document packed whole on one device after that piece; the last token of every device is a document of its own, and on the last device of a group its id is 16384. `routed_rows`: for each device the 48 indices are distinct and include 256 - 1; the first routed_count of them are ascending and name the routed tokens, at least one of them of sequence 0; the others are padding. `routed_count`: some device of every group uses all 48 slots.
All inputs are finite; a program needn't handle non-finite values.
Results may differ from the reference program's by a relative error of at most 0.012.
Values may be sent and summed in bfloat16 or wider, within the bound.
No kernel may reach another device: no remote copies, remote signals or barrier semaphores. Data moves between devices by JAX's collectives and lax.ppermute only.
A program may use at most 256 MiB of HBM per device.

```python
import jax
import jax.numpy as jnp
from jax import lax

D = 768
HEAD = 64
FF = 3072
TOK_DEV = 256
ROUTED_DEV = 48
GROUPS = 2
GROUP_TOKENS = 16384
N_SEQ = 64


def routing_plan(key):

    def one_group(group_key):
        keys_list = jax.random.split(group_key, 6)
        long_len = jax.random.randint(keys_list[0], (N_SEQ, 1), TOK_DEV // 4, TOK_DEV // 2 + 1).astype(jnp.int32)
        places = jnp.arange(TOK_DEV, dtype=jnp.int32)[None, :]
        starts = (jax.random.randint(keys_list[1], (N_SEQ, TOK_DEV), 0, 24) == 0) | (places == long_len) | (places == TOK_DEV - 1)
        start_pos = jnp.where(starts & (places >= long_len), places, 0)
        last_start = lax.cummax(start_pos, axis=1)
        devices_col = jnp.arange(N_SEQ, dtype=jnp.int32)[:, None]
        ids = jnp.where(places < long_len, 0, 1 + devices_col * TOK_DEV + last_start).astype(jnp.int32)
        counts = jax.random.randint(keys_list[2], (N_SEQ,), max(ROUTED_DEV // 3, 1), ROUTED_DEV + 1).astype(jnp.int32)
        full_device = jax.random.randint(keys_list[3], (), 0, N_SEQ)
        counts = jnp.where(jnp.arange(N_SEQ, dtype=jnp.int32) == full_device, ROUTED_DEV, counts).astype(jnp.int32)
        ranking = jax.random.randint(keys_list[4], (N_SEQ, TOK_DEV), 0, 1 << 16).astype(jnp.int32) * TOK_DEV + places
        forced = jax.random.randint(keys_list[5], (N_SEQ, 1), 0, long_len).astype(jnp.int32)
        ranking = jnp.where(places == TOK_DEV - 1, (1 << 16) * TOK_DEV + TOK_DEV - 1, ranking)
        ranking = jnp.where(places == forced, (1 << 16) * TOK_DEV + TOK_DEV, ranking)
        order = jnp.argsort(-ranking, axis=1)[:, :ROUTED_DEV].astype(jnp.int32)
        slot_ids = jnp.arange(ROUTED_DEV, dtype=jnp.int32)[None, :]
        keyed = jnp.sort(jnp.where(slot_ids < counts[:, None], order, order + TOK_DEV), axis=1)
        chosen = jnp.where(keyed >= TOK_DEV, keyed - TOK_DEV, keyed).astype(jnp.int32)
        return (ids.reshape(GROUP_TOKENS), chosen, counts)
    return jax.vmap(one_group)(jax.random.split(key, GROUPS))


def draw_seq_ids(key, part):
    return routing_plan(key)[0]


def draw_routed_rows(key, part):
    return routing_plan(key)[1]


def draw_routed_count(key, part):
    return routing_plan(key)[2]


def shard_levels(own_key, dims, cuts, least, largest):
    def one(axis_at, parts):
        draws = jax.random.uniform(jax.random.fold_in(jax.random.fold_in(own_key, 6), axis_at), (parts,), jnp.float32, least / len(cuts), largest / len(cuts))
        return jnp.repeat(jnp.exp(draws), dims[axis_at] // parts).reshape((-1,) + (1,) * (len(dims) - axis_at - 1))

    gain = one(*cuts[0])
    for cut in cuts[1:]:
        gain = gain * one(*cut)
    return gain


def gaussian(key, extent, width, most, pieces=(), held_as=jnp.bfloat16):
    gain = shard_levels(key, extent, pieces, -0.22, 0.18) if pieces else 1.0
    values = jax.random.normal(key, extent, jnp.float32) * width * gain
    return jnp.minimum(jnp.maximum(values, -most), most).astype(held_as)


def setup_inputs(seed: int = 0) -> dict:
    arg_keys = jax.random.split(jax.random.key(seed), 17)
    tokens = gaussian(arg_keys[0], (GROUPS, GROUP_TOKENS, D), 1.0, 6.0, ((0, 2), (1, 64)))
    router = gaussian(arg_keys[1], (D,), D ** -0.5, 0.21875, (), jnp.float32)
    gain_one = jnp.clip(1.0 + 0.1 * jax.random.normal(arg_keys[2], (D,), jnp.float32), 0.5, 1.5)
    bias_one = gaussian(arg_keys[3], (D,), 0.3, 1.8, (), jnp.float32)
    w_query = gaussian(arg_keys[4], (D, D), D ** -0.5, 0.21875)
    w_key = gaussian(arg_keys[5], (D, D), D ** -0.5, 0.21875)
    w_value = gaussian(arg_keys[6], (D, D), D ** -0.5, 0.21875)
    w_out = gaussian(arg_keys[7], (D, D), (D // 16) ** -0.5, 0.875)
    gain_two = jnp.clip(1.0 + 0.1 * jax.random.normal(arg_keys[8], (D,), jnp.float32), 0.5, 1.5)
    bias_two = gaussian(arg_keys[9], (D,), 0.3, 1.8, (), jnp.float32)
    w_expand = gaussian(arg_keys[10], (D, FF), D ** -0.5, 0.21875)
    w_contract = gaussian(arg_keys[11], (FF, D), FF ** -0.5, 0.109375)
    cotangent = gaussian(arg_keys[12], (GROUPS, GROUP_TOKENS, D), 1.0, 6.0, ((0, 2), (1, 64)))
    seq_ids = draw_seq_ids(jax.random.fold_in(arg_keys[16], 71), 0)
    routed_rows = draw_routed_rows(jax.random.fold_in(arg_keys[16], 71), 0)
    routed_count = draw_routed_count(jax.random.fold_in(arg_keys[16], 71), 0)
    return dict(tokens=tokens, router=router, gain_one=gain_one, bias_one=bias_one, w_query=w_query, w_key=w_key, w_value=w_value, w_out=w_out, gain_two=gain_two, bias_two=bias_two, w_expand=w_expand, w_contract=w_contract, cotangent=cotangent, seq_ids=seq_ids, routed_rows=routed_rows, routed_count=routed_count)


EPSILON = 1e-05
NEG_LARGE = -1e+30
EXACT_DOTS = lax.Precision.HIGHEST

@jax.custom_vjp
def low(v):
    return lax.optimization_barrier(v.astype(jnp.bfloat16)).astype(jnp.float32)

@jax.custom_vjp
def low_back(v):
    return v

def low_keep(v):
    return (low(v), None)

def low_pass(kept, grad):
    return (grad,)

def back_keep(v):
    return (v, None)

def back_low(kept, grad):
    return (low(grad),)
low.defvjp(low_keep, low_pass)
low_back.defvjp(back_keep, back_low)

def layer_norm(values_in, gain_vec, bias_vec):
    center = values_in - lax.optimization_barrier(jnp.mean(values_in, axis=-1, keepdims=True))
    spread = lax.optimization_barrier(jnp.mean(center * center, axis=-1, keepdims=True))
    return center * lax.rsqrt(spread + EPSILON) * gain_vec + bias_vec

def matmul(left, right):
    return jnp.dot(left, right, precision=EXACT_DOTS)

def block_rows(per_device, devices):
    factor = 1
    while factor * 2 * per_device <= 1024 and devices % (factor * 2) == 0:
        factor = factor * 2
    return factor * per_device

def group_block(x_group, seq_group, rows_group, count_group, weights):
    router, gain_one, bias_one, w_query, w_key, w_value, w_out, gain_two, bias_two, w_expand, w_contract = weights
    total = N_SEQ * ROUTED_DEV
    heads = D // HEAD
    scale = float(HEAD) ** (-0.5)
    offsets = (jnp.arange(N_SEQ, dtype=jnp.int32) * TOK_DEV)[:, None]
    positions = (offsets + rows_group.astype(jnp.int32)).reshape(total).astype(jnp.int32)
    is_valid = (jnp.arange(ROUTED_DEV, dtype=jnp.int32)[None, :] < count_group[:, None]).reshape(total)
    slot_ids = jnp.arange(total, dtype=jnp.int32)
    seq_rows = seq_group[positions]
    routed_x = x_group[positions]
    gate_value = jax.nn.sigmoid(matmul(routed_x, router))
    normed = low(layer_norm(routed_x, gain_one, bias_one))
    queries = low_back(low(matmul(normed, w_query))).reshape(total, heads, HEAD)
    keys_all = low_back(low(matmul(normed, w_key))).reshape(total, heads, HEAD)
    values_all = low_back(low(matmul(normed, w_value))).reshape(total, heads, HEAD)
    rows_block = block_rows(ROUTED_DEV, N_SEQ)

    def attend(block_id):
        start = block_id * rows_block
        q_block = lax.dynamic_slice_in_dim(queries, start, rows_block, 0)
        pos_block = lax.dynamic_slice_in_dim(positions, start, rows_block, 0)
        seq_block = lax.dynamic_slice_in_dim(seq_rows, start, rows_block, 0)
        slot_block = lax.dynamic_slice_in_dim(slot_ids, start, rows_block, 0)
        raw = low_back(jnp.einsum('qhd,khd->hqk', q_block, keys_all, precision=EXACT_DOTS))
        allowed = is_valid[None, :] & (seq_rows[None, :] == seq_block[:, None]) & (positions[None, :] <= pos_block[:, None]) | (slot_ids[None, :] == slot_block[:, None])
        scores = jnp.where(allowed[None], raw * scale, NEG_LARGE)
        probs = low(jax.nn.softmax(scores, axis=-1))
        return jnp.einsum('hqk,khd->qhd', probs, values_all, precision=EXACT_DOTS)
    blocks = lax.map(jax.checkpoint(attend), jnp.arange(total // rows_block, dtype=jnp.int32))
    mixed = low_back(low(blocks.reshape(total, D)))
    projected = low_back(matmul(mixed, w_out))
    hidden_one = routed_x + projected
    normed_two = low(layer_norm(hidden_one, gain_two, bias_two))
    expanded = low_back(matmul(normed_two, w_expand))
    activated = low(jax.nn.gelu(expanded, approximate=True))
    contracted = low_back(matmul(activated, w_contract))
    branch = projected + contracted
    scaled = jnp.where(is_valid, gate_value, 0.0)[:, None] * branch
    return x_group.at[positions].add(scaled)

def reference(tokens, router, gain_one, bias_one, w_query, w_key, w_value, w_out, gain_two, bias_two, w_expand, w_contract, cotangent, seq_ids, routed_rows, routed_count):
    weights = (router.astype(jnp.float32), gain_one.astype(jnp.float32), bias_one.astype(jnp.float32), w_query.astype(jnp.float32), w_key.astype(jnp.float32), w_value.astype(jnp.float32), w_out.astype(jnp.float32), gain_two.astype(jnp.float32), bias_two.astype(jnp.float32), w_expand.astype(jnp.float32), w_contract.astype(jnp.float32))

    def forward(x_float, *params):
        results = [group_block(x_float[group_id], seq_ids[group_id], routed_rows[group_id], routed_count[group_id], params) for group_id in range(GROUPS)]
        return jnp.stack(results)
    output, pull = jax.vjp(forward, tokens.astype(jnp.float32), *weights)
    grads = pull(cotangent.astype(jnp.float32))
    return (output.astype(jnp.bfloat16), grads[0].astype(jnp.bfloat16), grads[1], grads[2], grads[3], grads[4], grads[5], grads[6], grads[7], grads[8], grads[9], grads[10], grads[11])
```

```python
import jax
import jax.numpy as jnp
from jax import lax
from jax.experimental import pallas as pl
from jax.experimental.pallas import tpu as pltpu
from jax.sharding import Mesh
from jax.sharding import PartitionSpec as P

HEAD = 64
HEADS = 12
SLOTS = 48
D = 768
FF = 3072
TOK = 256
RUN = 384
EPSILON = 1e-05
NEG_LARGE = -1e30
EXACT = lax.Precision.HIGHEST
SCALE = float(HEAD) ** (-0.5)
F32 = jnp.float32
BF16 = jnp.bfloat16

SIXTEEN = ("yh", "z", "c")
SIZES = {"yh": 2, "x": 4, "z": 4, "c": 2, "yl": 2}


def width_of(axes):
    total = 1
    for axis in axes:
        total *= SIZES[axis]
    return total


def swap(parts, axes):
    return lax.all_to_all(parts, axes, split_axis=0, concat_axis=0, tiled=True)


def spread(part, axes):
    parts = width_of(axes)
    return swap(jnp.broadcast_to(part[None], (parts,) + part.shape), axes)


def gather_all(part):
    wide = spread(part, ("z",))
    wide = spread(wide, ("yh", "yl"))
    wide = spread(wide, ("x",))
    wide = spread(wide, ("c",))
    wide = wide.reshape((2, 4, 2, 2, 4) + part.shape)
    return jnp.moveaxis(wide, 0, 4)


def dot(left, right, dims, precision=None):
    return lax.dot_general(
        left, right, (dims, ((), ())), precision=precision, preferred_element_type=F32
    )


def mm(left, right):
    return dot(left, right, ((1,), (0,)))


def mm_tn(left, right):
    return dot(left, right, ((0,), (0,)))


def mm_nt(left, right):
    return dot(left, right, ((1,), (1,)))


def layer_norm(values_in, gain_vec, bias_vec):
    center = values_in - jnp.mean(values_in, axis=-1, keepdims=True)
    spread_ = jnp.mean(center * center, axis=-1, keepdims=True)
    inv = lax.rsqrt(spread_ + EPSILON)
    unit = center * inv
    return unit * gain_vec + bias_vec, unit, inv


def layer_norm_back(grad, unit, inv, gain_vec):
    scaled = grad * gain_vec
    mean_one = jnp.mean(scaled, axis=-1, keepdims=True)
    mean_two = jnp.mean(scaled * unit, axis=-1, keepdims=True)
    return inv * (scaled - mean_one - unit * mean_two)


def gelu_tanh(values_in):
    return jax.nn.gelu(values_in, approximate=True)


def attend_kernel(x_ref, q_ref, qcode_ref, kv_ref, kcode_ref, out_ref, lse_ref):
    x = x_ref[0]
    for run in range(2):
        q = q_ref[run]
        qcode = qcode_ref[run]

        def block(kb, carry, diagonal):
            peak, total, acc = carry
            yh = kb // 4
            xo = lax.rem(kb, 4)
            kv = kv_ref[xo, pl.ds(yh * RUN, RUN), :]
            kcode = kcode_ref[kb]
            scores = mm_nt(q, kv[:, :HEAD]) * SCALE
            allowed = qcode == kcode
            if diagonal:
                rows = lax.broadcasted_iota(jnp.int32, (RUN, RUN), 0)
                cols = lax.broadcasted_iota(jnp.int32, (RUN, RUN), 1)
                allowed = allowed & (cols <= rows)
            scores = jnp.where(allowed, scores, NEG_LARGE)
            new_peak = jnp.maximum(peak, jnp.max(scores, axis=1, keepdims=True))
            probs = jnp.exp(scores - new_peak)
            decay = jnp.exp(peak - new_peak)
            total = total * decay + jnp.sum(probs, axis=1, keepdims=True)
            acc = acc * decay + mm(probs.astype(BF16), kv[:, HEAD:])
            return new_peak, total, acc

        start = (
            jnp.full((RUN, 1), NEG_LARGE, F32),
            jnp.zeros((RUN, 1), F32),
            jnp.zeros((RUN, HEAD), F32),
        )
        last = 4 * run + x
        carry = block(last, start, True)
        peak, total, acc = lax.fori_loop(
            0, last, lambda kb, carry: block(kb, carry, False), carry
        )
        out_ref[run] = acc / total
        lse_ref[run] = peak + jnp.log(total)


def attend(x, q, qcode, kv, kcode):
    return pl.pallas_call(
        attend_kernel,
        out_shape=(
            jax.ShapeDtypeStruct((2, RUN, HEAD), F32),
            jax.ShapeDtypeStruct((2, RUN, 1), F32),
        ),
        in_specs=[pl.BlockSpec(memory_space=pltpu.SMEM)]
        + [pl.BlockSpec(memory_space=pltpu.VMEM)] * 4,
        out_specs=(pl.BlockSpec(memory_space=pltpu.VMEM),) * 2,
        compiler_params=pltpu.CompilerParams(vmem_limit_bytes=40 * 2**20),
        cost_estimate=pl.CostEstimate(
            flops=4 * 768 * 3072 * 64, bytes_accessed=3 * 2**20, transcendentals=768 * 3072
        ),
    )(x, q, qcode, kv, kcode)


def attend_back_kernel(
    x_ref, q_ref, do_ref, qcode_ref, lse_ref, inner_ref, kv_ref, kcode_ref, dq_ref, dkv_ref, acc_ref
):
    x = x_ref[0]
    acc_ref[...] = jnp.zeros_like(acc_ref)
    for run in range(2):
        q = q_ref[run]
        do = do_ref[run]
        qcode = qcode_ref[run]
        lse = lse_ref[run]
        inner = inner_ref[run]

        def block(kb, dq, diagonal):
            yh = kb // 4
            xo = lax.rem(kb, 4)
            kv = kv_ref[xo, pl.ds(yh * RUN, RUN), :]
            kcode = kcode_ref[kb]
            keys = kv[:, :HEAD]
            scores = mm_nt(keys, q) * SCALE
            allowed = qcode == kcode
            if diagonal:
                rows = lax.broadcasted_iota(jnp.int32, (RUN, RUN), 0)
                cols = lax.broadcasted_iota(jnp.int32, (RUN, RUN), 1)
                allowed = allowed & (rows <= cols)
            probs = jnp.where(allowed, jnp.exp(scores - lse), 0.0)
            grad_probs = mm_nt(kv[:, HEAD:], do)
            grad_raw = (probs * (grad_probs - inner) * SCALE).astype(BF16)
            dk = mm(grad_raw, q)
            dv = mm(probs.astype(BF16), do)
            acc_ref[kb] += jnp.concatenate([dk, dv], axis=1)
            return dq + mm_tn(keys, grad_raw)

        last = 4 * run + x
        dq = block(last, jnp.zeros((HEAD, RUN), F32), True)
        dq = lax.fori_loop(0, last, lambda kb, carry: block(kb, carry, False), dq)
        dq_ref[run] = dq
    for kb in range(8):
        dkv_ref[kb % 4, (kb // 4) * RUN : (kb // 4 + 1) * RUN, :] = acc_ref[kb].astype(BF16)


def attend_back(x, q, do, qcode, lse, inner, kv, kcode):
    return pl.pallas_call(
        attend_back_kernel,
        out_shape=(
            jax.ShapeDtypeStruct((2, HEAD, RUN), F32),
            jax.ShapeDtypeStruct((4, 2 * RUN, 2 * HEAD), BF16),
        ),
        in_specs=[pl.BlockSpec(memory_space=pltpu.SMEM)]
        + [pl.BlockSpec(memory_space=pltpu.VMEM)] * 7,
        out_specs=(pl.BlockSpec(memory_space=pltpu.VMEM),) * 2,
        scratch_shapes=[pltpu.VMEM((8, RUN, 2 * HEAD), F32)],
        compiler_params=pltpu.CompilerParams(vmem_limit_bytes=40 * 2**20),
        cost_estimate=pl.CostEstimate(
            flops=10 * 768 * 3072 * 64, bytes_accessed=6 * 2**20, transcendentals=768 * 3072
        ),
    )(x, q, do, qcode, lse, inner, kv, kcode)


def by_head(rows):
    parts = rows.reshape(SLOTS, HEADS, HEAD).transpose(1, 0, 2)
    return jnp.pad(parts, ((0, 4), (0, 0), (0, 0)))


def from_heads(parts):
    return parts[:HEADS].transpose(1, 0, 2).reshape(SLOTS, D)


def body(
    tokens,
    router,
    gain_one,
    bias_one,
    w_query,
    w_key,
    w_value,
    w_out,
    gain_two,
    bias_two,
    w_expand,
    w_contract,
    cotangent,
    seq_ids,
    routed_rows,
    routed_count,
):
    x_at = lax.axis_index("x")
    row_index = routed_rows[0, 0]
    routed_total = routed_count[0, 0]
    slot_ids = jnp.arange(SLOTS, dtype=jnp.int32)
    is_valid = slot_ids < routed_total
    x_local = tokens[0]
    picks = row_index[:, None] == jnp.arange(TOK, dtype=jnp.int32)[None, :]
    pick_low = picks.astype(BF16)
    pick_full = picks.astype(F32)
    routed_x = mm(pick_low, x_local)
    seq_rows = jnp.sum(jnp.where(picks, seq_ids[0][None, :], 0), axis=1)
    gate_value = jax.nn.sigmoid(jnp.sum(routed_x * router[None, :], axis=-1))
    normed, unit_one, inv_one = layer_norm(routed_x, gain_one, bias_one)
    normed_low = normed.astype(BF16)
    queries = mm(normed_low, w_query).astype(BF16)
    keys_own = mm(normed_low, w_key).astype(BF16)
    values_own = mm(normed_low, w_value).astype(BF16)

    same = (is_valid[None, :] & is_valid[:, None] & (seq_rows[None, :] == seq_rows[:, None])) | (
        slot_ids[None, :] == slot_ids[:, None]
    )
    first = jnp.min(jnp.where(same, slot_ids[None, :], SLOTS), axis=1)
    code = jnp.where(is_valid & (seq_rows == 0), 0, first + 1).astype(BF16)

    code_cols = jnp.pad(
        jnp.broadcast_to(code[None, :, None], (16, SLOTS, 1)), ((0, 0), (0, 0), (0, HEAD - 1))
    )
    to_heads = jnp.concatenate(
        [by_head(keys_own), by_head(values_own), by_head(queries), code_cols], axis=2
    )
    head_rows = swap(to_heads, SIXTEEN).reshape(2 * RUN, 4 * HEAD)
    normed_block = spread(normed_low, SIXTEEN).reshape(2 * RUN, D)
    codes_here = head_rows[:, 3 * HEAD].astype(F32)
    kv_here = jnp.concatenate(
        [head_rows[:, : 2 * HEAD], jnp.pad(codes_here.astype(BF16).reshape(6, 128), ((0, 10), (0, 0)))],
        axis=0,
    )
    kv_all = spread(kv_here, ("x",))
    q_here = head_rows[:, 2 * HEAD : 3 * HEAD].reshape(2, RUN, HEAD)

    def whole_codes(codes, x_of):
        local = jnp.arange(2 * RUN, dtype=jnp.int32)
        sixteen = local // SLOTS
        owner = (sixteen // 8) * 32 + x_of * 8 + lax.rem(sixteen, 8)
        return jnp.where(codes == 0, 0.0, codes + 64.0 * owner.astype(F32))

    q_codes = whole_codes(codes_here, x_at).reshape(2, RUN)
    k_codes = kv_all[:, 2 * RUN : 2 * RUN + 6, :].astype(F32).reshape(4, 2 * RUN)
    k_codes = jnp.stack([whole_codes(k_codes[i], i) for i in range(4)])
    k_codes = k_codes.reshape(4, 2, RUN).transpose(1, 0, 2).reshape(8, RUN)
    x_arr = x_at.astype(jnp.int32)[None]
    mixed_here, lse = attend(
        x_arr, q_here, q_codes[:, :, None], kv_all, k_codes[:, None, :]
    )
    mixed = from_heads(swap(mixed_here.astype(BF16).reshape(16, SLOTS, HEAD), SIXTEEN))

    projected = mm(mixed, w_out)
    hidden_one = routed_x + projected
    normed_two, unit_two, inv_two = layer_norm(hidden_one, gain_two, bias_two)
    normed_two_low = normed_two.astype(BF16)
    expanded = mm(normed_two_low, w_expand)
    activated, gelu_pull = jax.vjp(gelu_tanh, expanded)
    activated_low = activated.astype(BF16)
    contracted = mm(activated_low, w_contract)
    branch = projected + contracted
    gate_used = jnp.where(is_valid, gate_value, 0.0)
    output = (
        x_local.astype(F32)
        + dot(pick_full, gate_used[:, None] * branch, ((0,), (0,)), EXACT)
    ).astype(BF16)

    grad_local = cotangent[0]
    grad_rows = mm(pick_low, grad_local) * is_valid[:, None].astype(F32)
    grad_gate = jnp.sum(grad_rows * branch, axis=-1)
    grad_logit = grad_gate * gate_value * (1.0 - gate_value)
    grad_branch = gate_value[:, None] * grad_rows
    grad_contracted = grad_branch.astype(BF16)
    grad_activated = mm_nt(grad_contracted, w_contract)
    grad_expanded = gelu_pull(grad_activated)[0].astype(BF16)
    grad_normed_two = mm_nt(grad_expanded, w_expand)
    grad_hidden = layer_norm_back(grad_normed_two, unit_two, inv_two, gain_two)
    grad_gain_two = jnp.sum(grad_normed_two * unit_two, axis=0)
    grad_bias_two = jnp.sum(grad_normed_two, axis=0)
    grad_projected = (grad_branch + grad_hidden).astype(BF16)
    grad_mixed = mm_nt(grad_projected, w_out).astype(BF16)

    do_here = swap(by_head(grad_mixed), SIXTEEN).reshape(2, RUN, HEAD)
    inner = jnp.sum(do_here.astype(F32) * mixed_here, axis=-1)
    grad_q, grad_kv = attend_back(
        x_arr,
        q_here,
        do_here,
        q_codes[:, None, :],
        lse.reshape(2, 1, RUN),
        inner[:, None, :],
        kv_all,
        k_codes[:, :, None],
    )
    grad_kv_sum = jnp.sum(swap(grad_kv, ("x",)).astype(F32), axis=0).astype(BF16)
    grad_q_rows = grad_q.transpose(0, 2, 1).reshape(2 * RUN, HEAD).astype(BF16)
    grad_heads = jnp.concatenate([grad_kv_sum, grad_q_rows], axis=1)
    back = swap(
        jnp.pad(grad_heads, ((0, 0), (0, HEAD))).reshape(16, SLOTS, 4 * HEAD), SIXTEEN
    )
    grad_keys = from_heads(back[:, :, :HEAD])
    grad_values = from_heads(back[:, :, HEAD : 2 * HEAD])
    grad_queries = from_heads(back[:, :, 2 * HEAD : 3 * HEAD])

    grad_qkv = mm_tn(normed_block, grad_heads).astype(BF16)
    grad_qkv = jnp.sum(
        swap(grad_qkv.reshape(8, 96, 3 * HEAD), ("x", "yl")).astype(F32), axis=0
    ).astype(BF16)

    lefts = jnp.concatenate(
        [
            jnp.broadcast_to(normed_two_low[None], (4, SLOTS, D)),
            activated_low.reshape(SLOTS, 4, D).transpose(1, 0, 2),
        ]
    )
    rights = jnp.concatenate(
        [
            grad_expanded.reshape(SLOTS, 4, D).transpose(1, 0, 2),
            jnp.broadcast_to(grad_contracted[None], (4, SLOTS, D)),
        ]
    )
    mixed_parts = jnp.repeat(mixed.reshape(SLOTS, 2, 384).transpose(1, 0, 2), 4, axis=0)
    projected_parts = jnp.tile(grad_projected.reshape(SLOTS, 4, 192).transpose(1, 0, 2), (2, 1, 1))
    eight = swap(
        jnp.concatenate([lefts, rights, mixed_parts, projected_parts], axis=2), ("x", "c")
    ).reshape(8 * SLOTS, 2 * D + 576)
    unit_grad = mm_tn(eight[:, :D], eight[:, D : 2 * D]).astype(BF16)
    tile_grad = mm_tn(eight[:, 2 * D : 2 * D + 384], eight[:, 2 * D + 384 :]).astype(BF16)
    tile_grad = tile_grad.reshape(8, 48, 2, 96).transpose(0, 2, 1, 3).reshape(16, 48, 96)
    partial_grads = jnp.concatenate([unit_grad.reshape(16, 48, D), tile_grad], axis=2)
    own_grads = jnp.sum(
        swap(partial_grads, ("yh", "yl", "z")).astype(F32), axis=0
    ).astype(BF16)
    all_grads = gather_all(own_grads)
    all_grads = jnp.moveaxis(all_grads, 4, 1).reshape(8, 16, 48, 864)
    units = all_grads[:, :, :, :D].reshape(2, 4, D, D)
    final_expand = units[0].transpose(1, 0, 2).reshape(D, FF).astype(F32)
    final_contract = units[1].reshape(FF, D).astype(F32)
    tiles = all_grads[:, :, :, D:].reshape(2, 4, 8, 2, 48, 96)
    final_out = tiles.transpose(0, 2, 4, 1, 3, 5).reshape(D, D).astype(F32)

    all_qkv = gather_all(grad_qkv)
    all_qkv = all_qkv.transpose(1, 3, 4, 0, 2, 5, 6).reshape(16, D, 3 * HEAD)[:HEADS]
    all_qkv = all_qkv.transpose(1, 0, 2).astype(F32)
    final_key = all_qkv[:, :, :HEAD].reshape(D, D)
    final_value = all_qkv[:, :, HEAD : 2 * HEAD].reshape(D, D)
    final_query = all_qkv[:, :, 2 * HEAD :].reshape(D, D)

    grad_normed = (
        mm_nt(grad_queries, w_query) + mm_nt(grad_keys, w_key) + mm_nt(grad_values, w_value)
    )
    grad_norm_in = layer_norm_back(grad_normed, unit_one, inv_one, gain_one)
    grad_gain_one = jnp.sum(grad_normed * unit_one, axis=0)
    grad_bias_one = jnp.sum(grad_normed, axis=0)
    grad_router = jnp.sum(grad_logit[:, None] * routed_x, axis=0)
    grad_x_rows = grad_logit[:, None] * router[None, :] + grad_hidden + grad_norm_in
    input_grad = (
        grad_local.astype(F32) + dot(pick_full, grad_x_rows, ((0,), (0,)), EXACT)
    ).astype(BF16)
    vectors = jnp.stack(
        [grad_router, grad_gain_one, grad_bias_one, grad_gain_two, grad_bias_two]
        + [jnp.zeros((D,), F32)] * 3
    )
    vectors = jnp.sum(spread(vectors, SIXTEEN), axis=0)
    vectors = jnp.sum(spread(vectors, ("x", "yl")), axis=0)
    return (
        output[None],
        input_grad[None],
        vectors[0],
        vectors[1],
        vectors[2],
        final_query,
        final_key,
        final_value,
        final_out,
        vectors[3],
        vectors[4],
        final_expand,
        final_contract,
    )


def solution(mesh):
    fine = Mesh(mesh.devices.reshape(2, 4, 4, 2, 2), ("yh", "x", "z", "c", "yl"))
    seq = ("yh", "x", "z", "c")
    in_specs = (
        (P("yl", seq, None),)
        + (P(),) * 11
        + (P("yl", seq, None), P("yl", seq), P("yl", seq, None), P("yl", seq))
    )
    out_specs = (P("yl", seq, None),) * 2 + (P(),) * 11
    return jax.shard_map(body, mesh=fine, in_specs=in_specs, out_specs=out_specs, check_vma=False)
```

```python
import functools
import itertools

import jax
import jax.numpy as jnp
import numpy as np
from jax import lax
from jax.experimental import pallas as pl
from jax.experimental.pallas import tpu as pltpu
from jax.sharding import Mesh
from jax.sharding import PartitionSpec as P

HEAD = 64
HEADS = 12
SLOTS = 48
D = 768
FF = 3072
TOK = 256
RUN = 384
EPSILON = 1e-05
NEG_LARGE = -1e30
EXACT = lax.Precision.HIGHEST
SCALE = float(HEAD) ** (-0.5)
F32 = jnp.float32
BF16 = jnp.bfloat16

SIXTEEN = ("yh", "z", "c")
HOLDERS = [yh * 8 + z * 2 + c for c in range(2) for yh in range(2) for z in range(3)]
IDLE = [yh * 8 + 6 + c for yh in range(2) for c in range(2)]
SIZES = {"yh": 2, "x": 4, "z": 4, "c": 2, "yl": 2}


def width_of(axes):
    total = 1
    for axis in axes:
        total *= SIZES[axis]
    return total


def swap(parts, axes):
    return lax.all_to_all(parts, axes, split_axis=0, concat_axis=0, tiled=True)


def spread(part, axes):
    parts = width_of(axes)
    return swap(jnp.broadcast_to(part[None], (parts,) + part.shape), axes)


CHIPS = ("x", "yh", "yl", "z")
SMEM_SPEC = pl.BlockSpec(memory_space=pltpu.SMEM)
ANY_SPEC = pl.BlockSpec(memory_space=pl.ANY)
VMEM_SPEC = pl.BlockSpec(memory_space=pltpu.VMEM)
HBM_SPEC = pl.BlockSpec(memory_space=pltpu.HBM)


CUBE_AXES = ("x", "z", "c")
FIRST = (("x", "z"), ("z", "x"))


def ring_pairs(turn, step):
    pairs = []
    for x in range(4):
        for z in range(4):
            for c in range(2):
                to = {"x": x, "z": z}
                axis = FIRST[c][turn]
                to[axis] = (to[axis] + step) % 4
                pairs.append((x * 8 + z * 2 + c, to["x"] * 8 + to["z"] * 2 + c))
    return pairs


def ring_swap(parts, at, pairs_of, axes):
    mine = [lax.dynamic_index_in_dim(parts, at, 0, keepdims=False)]
    for step in (1, 2, 3):
        part = lax.dynamic_index_in_dim(parts, lax.rem(at + step, 4), 0, keepdims=False)
        mine.append(lax.ppermute(part, axes, pairs_of(step)))
    return mine


EVERY = ("yh", "x", "z", "c", "yl")
UNIT_ORDERS = (("x", "y", "z"), ("z", "x", "y"))


def gather_pairs(orders, stage, step):
    pairs = []
    for place in itertools.product(range(2), range(4), range(4), range(2), range(2)):
        yh, x, z, c, yl = place
        at = {"x": x, "y": yh * 2 + yl, "z": z}
        axis = orders[c][stage]
        at[axis] = (at[axis] + step) % 4
        source = (at["y"] // 2, at["x"], at["z"], c, at["y"] % 2)
        pairs.append(tuple(int(np.ravel_multi_index(p, (2, 4, 4, 2, 2))) for p in (source, place)))
    return pairs


def gather_step(part, orders, stage):
    return [part] + [
        lax.ppermute(part, EVERY, gather_pairs(orders, stage, step)) for step in (1, 2, 3)
    ]


def other_core(pieces):
    return [lax.ppermute(piece, "c", [(0, 1), (1, 0)]) for piece in pieces]


def chip_at(orders, core, me_ref, steps):
    at = {
        axis: (me_ref["xyz".index(axis)] + step) & 3
        for axis, step in zip(orders[core], steps, strict=True)
    }
    return at["x"], at["y"], at["z"]


def steps_to(orders, core, me_ref, chip):
    return [(chip["xyz".index(axis)] - me_ref["xyz".index(axis)]) & 3 for axis in orders[core]]


def dot(left, right, dims, precision=None):
    return lax.dot_general(
        left, right, (dims, ((), ())), precision=precision, preferred_element_type=F32
    )


def mm(left, right):
    return dot(left, right, ((1,), (0,)))


def mm_tn(left, right):
    return dot(left, right, ((0,), (0,)))


def mm_nt(left, right):
    return dot(left, right, ((1,), (1,)))


def layer_norm(values_in, gain_vec, bias_vec):
    center = values_in - jnp.mean(values_in, axis=-1, keepdims=True)
    spread_ = jnp.mean(center * center, axis=-1, keepdims=True)
    inv = lax.rsqrt(spread_ + EPSILON)
    unit = center * inv
    return unit * gain_vec + bias_vec, unit, inv


def layer_norm_back(grad, unit, inv, gain_vec):
    scaled = grad * gain_vec
    mean_one = jnp.mean(scaled, axis=-1, keepdims=True)
    mean_two = jnp.mean(scaled * unit, axis=-1, keepdims=True)
    return inv * (scaled - mean_one - unit * mean_two)


WIDE = 1216


def place_kernel(other, me_ref, *refs):
    pieces, refs = refs[:4], refs[4:]
    if other:
        sums_before_ref, vector_before_ref = refs[6:8]
        refs = refs[8:]
    (
        expand_ref, contract_ref, out_ref, key_ref, value_ref, query_ref, sums_ref, vector_ref,
        land_ref, stage_ref, tiles_ref, heads_ref, in_sems, out_sems,
    ) = refs

    def take(k3):
        return pltpu.make_async_copy(pieces[k3], land_ref.at[k3], in_sems.at[k3])

    for k3 in range(4):
        take(k3).start()

    def emit(core):
        for k3 in range(4):
            take(k3).wait()
            for k2 in range(4):
                for k1 in range(4):
                    x, y, z = chip_at(UNIT_ORDERS, core, me_ref, (k1, k2, k3))
                    staged = stage_ref.at[k3, k2 * 4 + k1]
                    staged[...] = land_ref[k3, k2, k1, :, :D].astype(F32)
                    if core == 0:
                        row = pl.multiple_of((z * 4 + y) * 48, 16)
                        cols = pl.ds(pl.multiple_of(x * D, D), D)
                        target = expand_ref.at[pl.ds(row, 48), cols]
                    else:
                        row = pl.multiple_of(z * D + (x * 4 + y) * 48, 16)
                        target = contract_ref.at[pl.ds(row, 48), :]
                    pltpu.make_async_copy(staged, target, out_sems.at[k3]).start()

        def shard(x, y, z, cols):
            k1, k2, k3 = steps_to(UNIT_ORDERS, core, me_ref, (x, y, z))
            return land_ref[k3, k2, k1, :, cols].astype(F32)

        def unit_shard(unit, at16, cols):
            if core == 0:
                return shard(unit, at16 % 4, at16 // 4, cols)
            return shard(at16 // 4, at16 % 4, unit, cols)

        for row in range(8):
            tiles_ref[row * 48 : (row + 1) * 48, :] = jnp.concatenate(
                [
                    unit_shard(unit, row * 2 + half, slice(D, 896))[:, :96]
                    for unit in range(4)
                    for half in range(2)
                ],
                axis=1,
            )
        rows = pl.ds(core * 384, 384)
        copies = [pltpu.make_async_copy(tiles_ref, out_ref.at[rows, :], out_sems.at[4])]
        copies[0].start()
        for at16 in range(16):
            total = sum(unit_shard(unit, at16, slice(D, 896)) for unit in range(4))
            if other:
                total += vector_before_ref[at16]
            vector_ref[at16] = total
        for x in range(4):
            for z in range(4):
                for yl in range(2):
                    halves = []
                    for yh in range(2):
                        block = shard(x, yh * 2 + yl, z, slice(896, WIDE))
                        halves.append(jnp.concatenate([block[:24], block[24:]], axis=1))
                    at = slice(((x * 4 + z) * 2 + yl) * 24, ((x * 4 + z) * 2 + yl + 1) * 24)
                    for kind in range(3):
                        cols = slice(kind * 192, (kind + 1) * 192)
                        heads_ref[kind, at, :] = jnp.concatenate(
                            [half[:, cols] for half in halves], axis=1
                        )
                    total = halves[0][:, 576:] + halves[1][:, 576:]
                    if other:
                        total += sums_before_ref[at, :]
                    sums_ref[at, :] = total
        cols = pl.ds(core * 384, 384)
        for kind, target in enumerate((key_ref, value_ref, query_ref)):
            copies.append(
                pltpu.make_async_copy(
                    heads_ref.at[kind], target.at[:, cols], out_sems.at[5 + kind]
                )
            )
            copies[-1].start()
        for k3 in range(4):
            held = stage_ref.at[k3]
            pltpu.make_async_copy(held, held, out_sems.at[k3]).wait()
        for copy in copies:
            copy.wait()

    for core in range(2):
        pl.when((me_ref[3] + other & 1) == core)(functools.partial(emit, core))


def place(me, pieces, before=None):
    before = () if before is None else tuple(before)
    return pl.pallas_call(
        functools.partial(place_kernel, 1 if before else 0),
        out_shape=(
            jax.ShapeDtypeStruct((D, FF), F32),
            jax.ShapeDtypeStruct((FF, D), F32),
        )
        + (jax.ShapeDtypeStruct((D, D), F32),) * 4
        + (jax.ShapeDtypeStruct((D, HEAD), F32), jax.ShapeDtypeStruct((16, 48, 128), F32)),
        in_specs=[SMEM_SPEC]
        + [ANY_SPEC] * 4
        + ([ANY_SPEC] * 6 + [VMEM_SPEC] * 2 if before else []),
        out_specs=(ANY_SPEC,) * 6 + (VMEM_SPEC,) * 2,
        scratch_shapes=[
            pltpu.VMEM((4, 4, 4, 48, WIDE), BF16),
            pltpu.VMEM((4, 16, 48, D), F32),
            pltpu.VMEM((384, D), F32),
            pltpu.VMEM((3, D, 384), F32),
            pltpu.SemaphoreType.DMA((4,)),
            pltpu.SemaphoreType.DMA((8,)),
        ],
        input_output_aliases={5 + i: i for i in range(6)} if before else {},
        compiler_params=pltpu.CompilerParams(vmem_limit_bytes=40 * 2**20),
        cost_estimate=pl.CostEstimate(flops=0, bytes_accessed=20 * 2**20, transcendentals=0),
    )(me, *pieces, *before)


def embed_kernel(
    count_ref, rows_ref, ids_ref, tokens_ref, gain_ref, bias_ref, wk_hbm, wv_hbm, wq_hbm,
    chunk_ref, normed_ref, routed_ref, w_ref, sems,
):
    for i, w in enumerate((wk_hbm, wv_hbm, wq_hbm)):
        pltpu.make_async_copy(w, w_ref.at[i], sems.at[i]).start()
    places = lax.broadcasted_iota(jnp.int32, (TOK, SLOTS), 0)
    picks = (rows_ref[...] == places).astype(F32).astype(BF16)
    routed = mm_tn(picks, tokens_ref[...])
    gain = gain_ref[...].reshape(1, D)
    bias = bias_ref[...].reshape(1, D)
    normed = layer_norm(routed, gain, bias)[0].astype(BF16)
    routed_ref[...] = routed
    normed_ref[...] = normed
    ids = ids_ref[...]
    halves = jnp.concatenate([ids >> 8, ids & 255] + [jnp.zeros((6, TOK), jnp.int32)], axis=0)
    halves = halves.astype(F32).astype(BF16)
    ids_rows = mm(halves, picks)
    ids_cols = dot(picks, halves, ((0,), (1,)))
    ids_row = ids_rows[0:1] * 256.0 + ids_rows[1:2]
    ids_col = ids_cols[:, 0:1] * 256.0 + ids_cols[:, 1:2]
    slot_row = lax.broadcasted_iota(jnp.int32, (SLOTS, SLOTS), 1)
    slot_col = lax.broadcasted_iota(jnp.int32, (SLOTS, SLOTS), 0)
    count = count_ref[0]
    same = (ids_row == ids_col) & (slot_row < count) & (slot_col < count) | (slot_row == slot_col)
    first = jnp.min(
        jnp.where(same, slot_row.astype(F32), float(SLOTS)), axis=1, keepdims=True
    )
    lanes = lax.broadcasted_iota(jnp.int32, (SLOTS, HEAD), 1)
    slots = lax.broadcasted_iota(jnp.int32, (SLOTS, HEAD), 0)
    is_long = (ids_col == 0.0) & (slots < count)
    marks = jnp.where(lanes == 0, first + 1.0, jnp.where(lanes == 1, count_ref[1] + 1.0, 0.0))
    marks = jnp.where(is_long, 0.0, marks).astype(BF16)
    parts = []
    for i in range(3):
        pltpu.make_async_copy((wk_hbm, wv_hbm, wq_hbm)[i], w_ref.at[i], sems.at[i]).wait()
        parts.append(mm(normed, w_ref[i]).astype(BF16))
    for head in range(HEADS):
        cols = slice(head * HEAD, (head + 1) * HEAD)
        chunk = jnp.concatenate([part[:, cols] for part in parts] + [marks], axis=1)
        for x in range(4):
            chunk_ref[x, HOLDERS[head]] = chunk
    for x in range(4):
        for holder in IDLE:
            chunk_ref[x, holder] = jnp.zeros((SLOTS, 4 * HEAD), BF16)


def embed(scalars, rows, ids, tokens, gain, bias, wk, wv, wq):
    return pl.pallas_call(
        embed_kernel,
        out_shape=(
            jax.ShapeDtypeStruct((4, 16, SLOTS, 4 * HEAD), BF16),
            jax.ShapeDtypeStruct((SLOTS, D), BF16),
            jax.ShapeDtypeStruct((SLOTS, D), F32),
        ),
        in_specs=[SMEM_SPEC] + [VMEM_SPEC] * 5 + [HBM_SPEC] * 3,
        out_specs=(VMEM_SPEC,) * 3,
        scratch_shapes=[pltpu.VMEM((3, D, D), BF16), pltpu.SemaphoreType.DMA((3,))],
        compiler_params=pltpu.CompilerParams(vmem_limit_bytes=58 * 2**20),
        cost_estimate=pl.CostEstimate(
            flops=6 * SLOTS * D * D, bytes_accessed=6 * 2**20, transcendentals=0
        ),
    )(scalars, rows, ids, tokens, gain, bias, wk, wv, wq)


def code_rows(recv_ref, codes_ref):
    lane = lax.broadcasted_iota(jnp.int32, (8, HEAD), 1)
    pick = jnp.where(lane == 0, 1.0, jnp.where(lane == 1, 64.0, 0.0)).astype(BF16)
    for kb in range(8):
        codes = mm_nt(pick, recv_ref[kb % 4, kb // 4, :, 3 * HEAD :])
        row = lax.broadcasted_iota(jnp.int32, (8, RUN), 0)
        codes_ref[kb] = jnp.where((row == 1) & (codes > 0.0), -1.0, codes)


def code_cols(block):
    marks = block[:, 3 * HEAD :].astype(F32)
    return marks[:, 0:1] + 64.0 * marks[:, 1:2]


def attend_kernel(x_ref, recv_ref, out_ref, low_ref, lse_ref, codes_ref):
    x = x_ref[0]
    code_rows(recv_ref, codes_ref)
    for run in range(2):
        own = recv_ref[x, run]
        q = own[:, 2 * HEAD : 3 * HEAD]
        qcode = code_cols(own)

        def block(kb, carry, diagonal):
            peak, total, acc = carry
            kv = recv_ref[lax.rem(kb, 4), kb // 4]
            scores = mm_nt(q, kv[:, :HEAD]) * SCALE
            if diagonal:
                rows = lax.broadcasted_iota(jnp.int32, (RUN, RUN), 0)
                cols = lax.broadcasted_iota(jnp.int32, (RUN, RUN), 1)
                allowed = (qcode == codes_ref[kb][0:1]) & (cols <= rows)
            else:
                allowed = qcode == codes_ref[kb][1:2]
            scores = jnp.where(allowed, scores, NEG_LARGE)
            new_peak = jnp.maximum(peak, jnp.max(scores, axis=1, keepdims=True))
            probs = jnp.exp(scores - new_peak)
            decay = jnp.exp(peak - new_peak)
            total = total * decay + jnp.sum(probs, axis=1, keepdims=True)
            acc = acc * decay + mm(probs.astype(BF16), kv[:, HEAD : 2 * HEAD])
            return new_peak, total, acc

        start = (
            jnp.full((RUN, 1), NEG_LARGE, F32),
            jnp.zeros((RUN, 1), F32),
            jnp.zeros((RUN, HEAD), F32),
        )
        last = 4 * run + x
        carry = block(last, start, True)
        peak, total, acc = lax.fori_loop(
            0, last, lambda kb, carry: block(kb, carry, False), carry
        )
        mixed = acc / total
        out_ref[run] = mixed
        low_ref[run, :, :HEAD] = mixed.astype(BF16)
        low_ref[run, :, HEAD:] = jnp.zeros((RUN, HEAD), BF16)
        lse_ref[run] = peak + jnp.log(total)


def attend(x, recv):
    return pl.pallas_call(
        attend_kernel,
        out_shape=(
            jax.ShapeDtypeStruct((2, RUN, HEAD), F32),
            jax.ShapeDtypeStruct((2, RUN, 2 * HEAD), BF16),
            jax.ShapeDtypeStruct((2, RUN, 1), F32),
        ),
        in_specs=[SMEM_SPEC, VMEM_SPEC],
        out_specs=(VMEM_SPEC,) * 3,
        scratch_shapes=[pltpu.VMEM((8, 8, RUN), F32)],
        compiler_params=pltpu.CompilerParams(vmem_limit_bytes=40 * 2**20),
        cost_estimate=pl.CostEstimate(
            flops=24 * 768 * 3072 * 64, bytes_accessed=3 * 2**20, transcendentals=768 * 3072
        ),
    )(x, recv)


def attend_back_kernel(
    x_ref, recv_ref, do_ref, mixed_ref, lse_ref, dq_ref, dkv_ref, codes_ref, acc_ref
):
    x = x_ref[0]
    acc_ref[...] = jnp.zeros_like(acc_ref)
    code_rows(recv_ref, codes_ref)
    for run in range(2):
        q = recv_ref[x, run][:, 2 * HEAD : 3 * HEAD]
        do = do_ref[run][:, :HEAD]
        last = 4 * run + x
        qcodes = codes_ref[last]
        lse = lse_ref[run]
        inner = dot(
            jnp.ones((8, HEAD), F32), do.astype(F32) * mixed_ref[run], ((1,), (1,)), EXACT
        )[0:1]

        def block(kb, dq, diagonal):
            kv = recv_ref[lax.rem(kb, 4), kb // 4]
            keys = kv[:, :HEAD]
            kcode = code_cols(kv)
            scores = mm_nt(keys, q) * SCALE
            if diagonal:
                rows = lax.broadcasted_iota(jnp.int32, (RUN, RUN), 0)
                cols = lax.broadcasted_iota(jnp.int32, (RUN, RUN), 1)
                allowed = (kcode == qcodes[0:1]) & (rows <= cols)
            else:
                allowed = kcode == qcodes[1:2]
            probs = jnp.where(allowed, jnp.exp(scores - lse), 0.0)
            grad_probs = mm_nt(kv[:, HEAD : 2 * HEAD], do)
            grad_raw = (probs * (grad_probs - inner) * SCALE).astype(BF16)
            dk = mm(grad_raw, q)
            dv = mm(probs.astype(BF16), do)
            acc_ref[kb] += jnp.concatenate([dk, dv], axis=1)
            return dq + mm_tn(keys, grad_raw)

        dq = block(last, jnp.zeros((HEAD, RUN), F32), True)
        dq = lax.fori_loop(0, last, lambda kb, carry: block(kb, carry, False), dq)
        dq_ref[run] = dq.T.astype(BF16)
    for kb in range(8):
        dkv_ref[kb % 4, kb // 4] = acc_ref[kb].astype(BF16)


def attend_back(x, recv, do, mixed, lse):
    return pl.pallas_call(
        attend_back_kernel,
        out_shape=(
            jax.ShapeDtypeStruct((2, RUN, HEAD), BF16),
            jax.ShapeDtypeStruct((4, 2, RUN, 2 * HEAD), BF16),
        ),
        in_specs=[SMEM_SPEC] + [VMEM_SPEC] * 4,
        out_specs=(VMEM_SPEC,) * 2,
        scratch_shapes=[pltpu.VMEM((8, 8, RUN), F32), pltpu.VMEM((8, RUN, 2 * HEAD), F32)],
        compiler_params=pltpu.CompilerParams(vmem_limit_bytes=40 * 2**20),
        cost_estimate=pl.CostEstimate(
            flops=60 * 768 * 3072 * 64, bytes_accessed=6 * 2**20, transcendentals=768 * 3072
        ),
    )(x, recv, do, mixed, lse)


ROOT = 0.7978845608028654
CUBE = 0.044715


def feed_kernel(
    parts_ref, routed_ref, gate_ref, branch_ref, low_ref, grad_act_ref, gain_ref, bias_ref,
    core_ref, wo_hbm, we_hbm,
    kept_ref, given_ref, back_ref, projected_ref, hidden_ref, logit_ref, vector_ref, act_ref,
    wo_ref, we_ref, sems,
):
    copies = [pltpu.make_async_copy(wo_hbm, wo_ref, sems.at[4])]
    for i in range(4):
        cols = pl.ds(i * D, D)
        copies.append(pltpu.make_async_copy(we_hbm.at[:, cols], we_ref.at[i], sems.at[i]))
    for copy in copies:
        copy.start()
    mixed = jnp.concatenate([parts_ref[holder, :, :HEAD] for holder in HOLDERS], axis=1)
    copies[0].wait()
    projected = mm(mixed, wo_ref[...])
    projected_ref[...] = projected
    routed = routed_ref[...]
    gain = gain_ref[...]
    normed, unit, inv = layer_norm(routed + projected, gain, bias_ref[...])
    normed = normed.astype(BF16)
    grad_branch = branch_ref[...]
    grad_contracted = low_ref[...]
    grad_normed = jnp.zeros((SLOTS, D), F32)
    inner = jnp.sum(grad_branch * projected, axis=1, keepdims=True)
    for i in range(4):
        copies[i + 1].wait()
        v = mm(normed, we_ref[i])
        t = jnp.tanh(ROOT * (v + CUBE * v * v * v))
        half = 0.5 * (1.0 + t)
        act = v * half
        slope = half + 0.5 * v * (1.0 - t * t) * (ROOT * (1.0 + 3.0 * CUBE * v * v))
        grad_act = grad_act_ref[:, i * D : (i + 1) * D]
        inner += jnp.sum(act * grad_act, axis=1, keepdims=True)
        act = act.astype(BF16)
        grad_expanded = (grad_act * slope).astype(BF16)
        grad_normed += mm_nt(grad_expanded, we_ref[i])
        act_ref[:, i * D : (i + 1) * D] = act

        @pl.when(core_ref[0] == 0)
        def _(i=i, grad_expanded=grad_expanded, act=act):
            kept_ref[i, :, :D] = normed
            kept_ref[i, :, D : 2 * D] = grad_expanded
            given_ref[i, :, :D] = act
            given_ref[i, :, D : 2 * D] = grad_contracted

        @pl.when(core_ref[0] == 1)
        def _(i=i, grad_expanded=grad_expanded, act=act):
            given_ref[i, :, :D] = normed
            given_ref[i, :, D : 2 * D] = grad_expanded
            kept_ref[i, :, :D] = act
            kept_ref[i, :, D : 2 * D] = grad_contracted
    grad_logit = (1.0 - gate_ref[...]) * inner
    logit_ref[...] = grad_logit
    grad_hidden = layer_norm_back(grad_normed, unit, inv, gain)
    hidden_ref[...] = grad_hidden
    grad_projected = (grad_branch + grad_hidden).astype(BF16)
    grad_mixed = mm_nt(grad_projected, wo_ref[...]).astype(BF16)
    for head in range(HEADS):
        back_ref[HOLDERS[head], :, :HEAD] = grad_mixed[:, head * HEAD : (head + 1) * HEAD]
        back_ref[HOLDERS[head], :, HEAD:] = jnp.zeros((SLOTS, HEAD), BF16)
    for holder in IDLE:
        back_ref[holder] = jnp.zeros((SLOTS, 2 * HEAD), BF16)
    halves = (mixed[:, :384], mixed[:, 384:])
    for i in range(4):
        part = grad_projected[:, i * 192 : (i + 1) * 192]
        kept_ref[i, :, 2 * D + 384 :] = part
        given_ref[i, :, 2 * D + 384 :] = part
    for core in range(2):

        @pl.when(core_ref[0] == core)
        def _(core=core):
            for i in range(4):
                kept_ref[i, :, 2 * D : 2 * D + 384] = halves[core]
                given_ref[i, :, 2 * D : 2 * D + 384] = halves[1 - core]

    vector_ref[0:1] = jnp.sum(grad_logit * routed, axis=0, keepdims=True)
    vector_ref[1:2] = jnp.sum(grad_normed * unit, axis=0, keepdims=True)
    vector_ref[2:3] = jnp.sum(grad_normed, axis=0, keepdims=True)


def feed(parts, routed, gate, branch, low, grad_act, gain, bias, core, wo, we):
    return pl.pallas_call(
        feed_kernel,
        out_shape=(
            jax.ShapeDtypeStruct((4, SLOTS, 2 * D + 576), BF16),
            jax.ShapeDtypeStruct((4, SLOTS, 2 * D + 576), BF16),
            jax.ShapeDtypeStruct((16, SLOTS, 2 * HEAD), BF16),
            jax.ShapeDtypeStruct((SLOTS, D), F32),
            jax.ShapeDtypeStruct((SLOTS, D), F32),
            jax.ShapeDtypeStruct((SLOTS, 1), F32),
            jax.ShapeDtypeStruct((3, D), F32),
            jax.ShapeDtypeStruct((SLOTS, FF), BF16),
        ),
        in_specs=[VMEM_SPEC] * 8 + [SMEM_SPEC] + [HBM_SPEC] * 2,
        out_specs=(VMEM_SPEC,) * 8,
        scratch_shapes=[
            pltpu.VMEM((D, D), BF16),
            pltpu.VMEM((4, D, D), BF16),
            pltpu.SemaphoreType.DMA((5,)),
        ],
        compiler_params=pltpu.CompilerParams(vmem_limit_bytes=58 * 2**20),
        cost_estimate=pl.CostEstimate(
            flops=20 * SLOTS * D * D, bytes_accessed=10 * 2**20, transcendentals=SLOTS * FF
        ),
    )(parts, routed, gate, branch, low, grad_act, gain, bias, core, wo, we)


def unit_kernel(*refs):
    parts, (vector_ref, out_ref) = refs[:4], refs[4:]

    def outer(left, right):
        total = jnp.zeros((left.stop - left.start, right.stop - right.start), F32)
        for part in parts:
            total += mm_tn(part[:, left], part[:, right])
        return total.astype(BF16)

    tile = outer(slice(2 * D, 2 * D + 384), slice(2 * D + 384, 2 * D + 576))
    for block in range(2):
        unit = outer(slice(block * 384, (block + 1) * 384), slice(D, 2 * D))
        for i in range(8):
            at = block * 8 + i
            out_ref[at // 4, at % 4, :, :D] = unit[i * 48 : (i + 1) * 48]
            out_ref[at // 4, at % 4, :, D:] = jnp.concatenate(
                [
                    tile[(at // 2) * 48 : (at // 2 + 1) * 48, (at % 2) * 96 : (at % 2 + 1) * 96],
                    vector_ref[at],
                ],
                axis=1,
            )


def unit_grads(parts, vectors):
    return pl.pallas_call(
        unit_kernel,
        out_shape=jax.ShapeDtypeStruct((4, 4, 48, 896), BF16),
        in_specs=[VMEM_SPEC] * 5,
        out_specs=VMEM_SPEC,
        compiler_params=pltpu.CompilerParams(vmem_limit_bytes=24 * 2**20),
        cost_estimate=pl.CostEstimate(
            flops=2 * 384 * D * D, bytes_accessed=3 * 2**20, transcendentals=0
        ),
    )(*parts, vectors)


def embed_back_kernel(
    back_ref, routed_ref, hidden_ref, logit_ref, rows_ref, grad_ref, router_ref, gain_ref,
    wk_hbm, wv_hbm, wq_hbm, out_ref, w_ref, sems,
):
    copies = [
        pltpu.make_async_copy(w, w_ref.at[i], sems.at[i])
        for i, w in enumerate((wk_hbm, wv_hbm, wq_hbm))
    ]
    for copy in copies:
        copy.start()
    routed = routed_ref[...]
    gain = gain_ref[...].reshape(1, D)
    unused, unit, inv = layer_norm(routed, gain, 0.0)
    grad_normed = jnp.zeros((SLOTS, D), F32)
    for i in range(3):
        grads = jnp.concatenate(
            [back_ref[holder, :, i * HEAD : (i + 1) * HEAD] for holder in HOLDERS], axis=1
        )
        copies[i].wait()
        grad_normed += mm_nt(grads, w_ref[i])
    grad_rows = (
        logit_ref[...] * router_ref[...].reshape(1, D)
        + hidden_ref[...]
        + layer_norm_back(grad_normed, unit, inv, gain)
    )
    places = lax.broadcasted_iota(jnp.int32, (TOK, SLOTS), 0)
    picks = (rows_ref[...] == places).astype(F32)
    out_ref[...] = (
        grad_ref[...].astype(F32) + dot(picks, grad_rows, ((1,), (0,)), EXACT)
    ).astype(BF16)


def embed_back(back, routed, hidden, logit, rows, grad, router, gain, wk, wv, wq):
    return pl.pallas_call(
        embed_back_kernel,
        out_shape=jax.ShapeDtypeStruct((TOK, D), BF16),
        in_specs=[VMEM_SPEC] * 8 + [HBM_SPEC] * 3,
        out_specs=VMEM_SPEC,
        scratch_shapes=[pltpu.VMEM((3, D, D), BF16), pltpu.SemaphoreType.DMA((3,))],
        compiler_params=pltpu.CompilerParams(vmem_limit_bytes=58 * 2**20),
        cost_estimate=pl.CostEstimate(
            flops=6 * SLOTS * D * D, bytes_accessed=6 * 2**20, transcendentals=0
        ),
    )(back, routed, hidden, logit, rows, grad, router, gain, wk, wv, wq)


def body(
    tokens,
    router,
    gain_one,
    bias_one,
    w_query,
    w_key,
    w_value,
    w_out,
    gain_two,
    bias_two,
    w_expand,
    w_contract,
    cotangent,
    seq_ids,
    routed_rows,
    routed_count,
):
    x_at = lax.axis_index("x").astype(jnp.int32)
    core_at = lax.axis_index("c").astype(jnp.int32)
    y_at = lax.axis_index(("yh", "yl")).astype(jnp.int32)
    z_at = lax.axis_index("z").astype(jnp.int32)
    first_at = jnp.where(core_at == 0, x_at, z_at)
    second_at = jnp.where(core_at == 0, z_at, x_at)
    row_index = routed_rows[0, 0]
    routed_total = routed_count[0, 0]
    x_local = tokens[0]
    place_at = lax.axis_index(("z", "c")).astype(jnp.int32)
    to_heads, normed_low, routed_x = embed(
        jnp.stack([routed_total, place_at]),
        routed_rows[0],
        seq_ids,
        x_local,
        gain_one,
        bias_one,
        w_key,
        w_value,
        w_query,
    )
    recv = swap(to_heads.reshape(64, SLOTS, 4 * HEAD), ("x",) + SIXTEEN)
    recv = recv.reshape(4, 2, RUN, 4 * HEAD)
    normed_block = lax.all_gather(normed_low, SIXTEEN, axis=0, tiled=True)

    is_valid = jnp.arange(SLOTS, dtype=jnp.int32) < routed_total
    picks = row_index[:, None] == jnp.arange(TOK, dtype=jnp.int32)[None, :]
    pick_low = picks.astype(BF16)
    pick_full = picks.astype(F32)
    gate_value = jax.nn.sigmoid(jnp.sum(routed_x * router[None, :], axis=-1))
    gate_used = jnp.where(is_valid, gate_value, 0.0)
    grad_local = cotangent[0]
    grad_branch = gate_used[:, None] * mm(pick_low, grad_local)
    grad_contracted = grad_branch.astype(BF16)
    grad_activated = mm_nt(grad_contracted, w_contract)

    mixed_here, mixed_low, lse = attend(x_at[None], recv)
    mixed_parts = swap(mixed_low.reshape(16, SLOTS, 2 * HEAD), SIXTEEN)
    (kept, given, do_parts, projected, grad_hidden, grad_logit, vectors, activated_low) = feed(
        mixed_parts,
        routed_x,
        gate_value[:, None],
        grad_branch,
        grad_contracted,
        grad_activated,
        gain_two[None],
        bias_two[None],
        core_at[None],
        w_out,
        w_expand,
    )
    given = lax.ppermute(given, "c", [(0, 1), (1, 0)])
    eight = jnp.concatenate([kept, given], axis=1)
    eight = ring_swap(eight, first_at, lambda step: ring_pairs(0, step), CUBE_AXES)
    do_parts = swap(do_parts, SIXTEEN)
    eight, do_parts, normed_block = lax.optimization_barrier((eight, do_parts, normed_block))
    vectors = jnp.pad(vectors.astype(BF16).reshape(16, 48, 3), ((0, 0), (0, 0), (0, 29)))
    partial_grads = unit_grads(eight, vectors)
    grad_q, grad_kv = attend_back(
        x_at[None], recv, do_parts.reshape(2, RUN, 2 * HEAD), mixed_here, lse.reshape(2, 1, RUN)
    )
    grad_kv = swap(grad_kv, ("x",))
    partial_grads = ring_swap(
        partial_grads, second_at, lambda step: ring_pairs(1, step), CUBE_AXES
    )
    partial_grads = sum(part.astype(F32) for part in partial_grads).astype(BF16)
    partial_grads = ring_swap(
        partial_grads,
        y_at,
        lambda step: [(i, (i + step) % 4) for i in range(4)],
        ("yh", "yl"),
    )
    own_grads = sum(part.astype(F32) for part in partial_grads).astype(BF16)

    branch = projected + mm(activated_low, w_contract)
    output = (
        x_local.astype(F32)
        + dot(pick_full, gate_used[:, None] * branch, ((0,), (0,)), EXACT)
    ).astype(BF16)
    grad_kv, output = lax.optimization_barrier((grad_kv, output))
    grad_kv_sum = jnp.sum(grad_kv.astype(F32), axis=0).astype(BF16)
    grad_heads = jnp.concatenate(
        [grad_kv_sum.reshape(2 * RUN, 2 * HEAD), grad_q.reshape(2 * RUN, HEAD)], axis=1
    )

    grad_qkv = mm_tn(normed_block, grad_heads).astype(BF16).reshape(32, 24, 3 * HEAD)
    column_sum = jnp.sum(grad_heads.astype(F32), axis=0).astype(BF16)
    column_sum = jnp.broadcast_to(column_sum[None, None, :], (32, 8, 3 * HEAD))
    grad_qkv = swap(jnp.concatenate([grad_qkv, column_sum], axis=1), ("x", "z", "yl"))
    grad_qkv = jnp.sum(grad_qkv.reshape(4, 4, 2, 32, 3 * HEAD)[:, :3].astype(F32), axis=(0, 2))
    grad_qkv = jnp.concatenate(
        [
            grad_qkv[:, :, kind * HEAD : (kind + 1) * HEAD].transpose(1, 0, 2).reshape(32, 3 * HEAD)
            for kind in range(3)
        ],
        axis=1,
    )
    column_sum = grad_qkv[24]
    grad_qkv = grad_qkv[:24]
    w_part = jnp.concatenate(
        [
            lax.dynamic_slice(
                w,
                (lax.axis_index(("x", "z", "yl")) * 24, (core_at * 2 + lax.axis_index("yh")) * 3 * HEAD),
                (24, 3 * HEAD),
            )
            for w in (w_key, w_value, w_query)
        ],
        axis=1,
    ).astype(F32)
    norm_sums = jnp.stack(
        [jnp.sum(w_part * grad_qkv, axis=1), jnp.sum(w_part * column_sum[None, :], axis=1)], axis=1
    )
    own_qkv = jnp.concatenate([grad_qkv, jnp.pad(norm_sums, ((0, 0), (0, 62)))], axis=1)
    own_qkv = jnp.concatenate([own_qkv[:, :320], own_qkv[:, 320:]], axis=0).astype(BF16)
    shards = jnp.concatenate([own_grads, own_qkv], axis=1)
    back = swap(
        jnp.pad(grad_heads, ((0, 0), (0, HEAD))).reshape(16, SLOTS, 4 * HEAD), SIXTEEN
    )
    shards = gather_step(shards, UNIT_ORDERS, 0)
    shards, back = lax.optimization_barrier((shards, back))
    shards = gather_step(jnp.stack(shards), UNIT_ORDERS, 1)
    shards = gather_step(jnp.stack(shards), UNIT_ORDERS, 2)
    input_grad = embed_back(
        back,
        routed_x,
        grad_hidden,
        grad_logit,
        routed_rows[0],
        grad_local,
        router,
        gain_one,
        w_key,
        w_value,
        w_query,
    )
    shards[2], input_grad = lax.optimization_barrier((shards[2], input_grad))
    me = jnp.stack([x_at, y_at, z_at, core_at])
    placed = place(me, shards)
    placed = place(me, other_core(shards), placed)
    final_expand, final_contract, final_out, final_key, final_value, final_query = placed[:6]
    norm_sums = placed[6][:, :2].T
    grad_gain_one = (norm_sums[0] - bias_one * norm_sums[1]) / gain_one
    grad_bias_one = norm_sums[1]
    vectors = placed[7][:, :, 96:]
    vectors = vectors[:, :, :3].reshape(3, D)
    return (
        output[None],
        input_grad[None],
        vectors[0],
        grad_gain_one,
        grad_bias_one,
        final_query,
        final_key,
        final_value,
        final_out,
        vectors[1],
        vectors[2],
        final_expand,
        final_contract,
    )


def solution(mesh):
    fine = Mesh(mesh.devices.reshape(2, 4, 4, 2, 2), ("yh", "x", "z", "c", "yl"))
    seq = ("yh", "x", "z", "c")
    in_specs = (
        (P("yl", seq, None),)
        + (P(),) * 11
        + (P("yl", seq, None), P("yl", seq), P("yl", seq, None), P("yl", seq))
    )
    out_specs = (P("yl", seq, None),) * 2 + (P(),) * 11
    return jax.shard_map(body, mesh=fine, in_specs=in_specs, out_specs=out_specs, check_vma=False)
```

```python
import functools
import itertools

import jax
import jax.numpy as jnp
import numpy as np
from jax import lax
from jax.experimental import pallas as pl
from jax.experimental.pallas import tpu as pltpu
from jax.sharding import Mesh
from jax.sharding import PartitionSpec as P

HEAD = 64
HEADS = 12
SLOTS = 48
D = 768
FF = 3072
TOK = 256
RUN = 384
EPSILON = 1e-05
NEG_LARGE = -1e30
EXACT = lax.Precision.HIGHEST
SCALE = float(HEAD) ** (-0.5)
F32 = jnp.float32
BF16 = jnp.bfloat16

SIXTEEN = ("yh", "z", "c")
HOLDERS = [yh * 8 + z * 2 + c for c in range(2) for yh in range(2) for z in range(3)]
IDLE = [yh * 8 + 6 + c for yh in range(2) for c in range(2)]
SIZES = {"yh": 2, "x": 4, "z": 4, "c": 2, "yl": 2}


def width_of(axes):
    total = 1
    for axis in axes:
        total *= SIZES[axis]
    return total


def swap(parts, axes):
    return lax.all_to_all(parts, axes, split_axis=0, concat_axis=0, tiled=True)


def spread(part, axes):
    parts = width_of(axes)
    return swap(jnp.broadcast_to(part[None], (parts,) + part.shape), axes)


CHIPS = ("x", "yh", "yl", "z")
SMEM_SPEC = pl.BlockSpec(memory_space=pltpu.SMEM)
ANY_SPEC = pl.BlockSpec(memory_space=pl.ANY)
VMEM_SPEC = pl.BlockSpec(memory_space=pltpu.VMEM)
HBM_SPEC = pl.BlockSpec(memory_space=pltpu.HBM)


CUBE_AXES = ("x", "z", "c")
FIRST = (("x", "z"), ("z", "x"))


def ring_pairs(turn, step):
    pairs = []
    for x in range(4):
        for z in range(4):
            for c in range(2):
                to = {"x": x, "z": z}
                axis = FIRST[c][turn]
                to[axis] = (to[axis] + step) % 4
                pairs.append((x * 8 + z * 2 + c, to["x"] * 8 + to["z"] * 2 + c))
    return pairs


def ring_swap(parts, at, pairs_of, axes):
    mine = [lax.dynamic_index_in_dim(parts, at, 0, keepdims=False)]
    for step in (1, 2, 3):
        part = lax.dynamic_index_in_dim(parts, lax.rem(at + step, 4), 0, keepdims=False)
        mine.append(lax.ppermute(part, axes, pairs_of(step)))
    return mine


EVERY = ("yh", "x", "z", "c", "yl")
UNIT_ORDERS = (("x", "y", "z"), ("z", "x", "y"))


def gather_pairs(orders, stage, step):
    pairs = []
    for place in itertools.product(range(2), range(4), range(4), range(2), range(2)):
        yh, x, z, c, yl = place
        at = {"x": x, "y": yh * 2 + yl, "z": z}
        axis = orders[c][stage]
        at[axis] = (at[axis] + step) % 4
        source = (at["y"] // 2, at["x"], at["z"], c, at["y"] % 2)
        pairs.append(tuple(int(np.ravel_multi_index(p, (2, 4, 4, 2, 2))) for p in (source, place)))
    return pairs


def gather_step(part, orders, stage):
    return [part] + [
        lax.ppermute(part, EVERY, gather_pairs(orders, stage, step)) for step in (1, 2, 3)
    ]


def other_core(pieces):
    return [lax.ppermute(piece, "c", [(0, 1), (1, 0)]) for piece in pieces]


def chip_at(orders, core, me_ref, steps):
    at = {
        axis: (me_ref["xyz".index(axis)] + step) & 3
        for axis, step in zip(orders[core], steps, strict=True)
    }
    return at["x"], at["y"], at["z"]


def steps_to(orders, core, me_ref, chip):
    return [(chip["xyz".index(axis)] - me_ref["xyz".index(axis)]) & 3 for axis in orders[core]]


def dot(left, right, dims, precision=None):
    return lax.dot_general(
        left, right, (dims, ((), ())), precision=precision, preferred_element_type=F32
    )


def mm(left, right):
    return dot(left, right, ((1,), (0,)))


def mm_tn(left, right):
    return dot(left, right, ((0,), (0,)))


def mm_nt(left, right):
    return dot(left, right, ((1,), (1,)))


def layer_norm(values_in, gain_vec, bias_vec):
    center = values_in - jnp.mean(values_in, axis=-1, keepdims=True)
    spread_ = jnp.mean(center * center, axis=-1, keepdims=True)
    inv = lax.rsqrt(spread_ + EPSILON)
    unit = center * inv
    return unit * gain_vec + bias_vec, unit, inv


def layer_norm_back(grad, unit, inv, gain_vec):
    scaled = grad * gain_vec
    mean_one = jnp.mean(scaled, axis=-1, keepdims=True)
    mean_two = jnp.mean(scaled * unit, axis=-1, keepdims=True)
    return inv * (scaled - mean_one - unit * mean_two)


def place_kernel(other, me_ref, *refs):
    units_in, pieces, refs = refs[0], refs[1:5], refs[5:]
    if other:
        refs = refs[6:]
    (
        expand_ref, contract_ref, out_ref, key_ref, value_ref, query_ref, sums_ref, vector_ref,
        land_ref, land_heads_ref, stage_ref, tiles_ref, heads_ref, in_sems, out_sems,
    ) = refs

    def take(i):
        if i < 4:
            rows = pl.ds(i * 16, 16)
            return pltpu.make_async_copy(units_in.at[rows], land_ref.at[rows], in_sems.at[i])
        return pltpu.make_async_copy(pieces[i - 4], land_heads_ref.at[i - 4], in_sems.at[i])

    for i in range(8):
        take(i).start()

    def emit(core):
        for x in range(4):
            take(x).wait()
            for y in range(4):
                for z in range(4):
                    at = x * 16 + y * 4 + z
                    staged = stage_ref.at[x, y * 4 + z]
                    staged[...] = land_ref[at, :, :D].astype(F32)
                    if core == 0:
                        row = (z * 4 + y) * 48
                        cols = pl.ds(x * D, D)
                        target = expand_ref.at[pl.ds(row, 48), cols]
                    else:
                        row = z * D + (x * 4 + y) * 48
                        target = contract_ref.at[pl.ds(row, 48), :]
                    pltpu.make_async_copy(staged, target, out_sems.at[x]).start()

        def unit_shard(unit, at16, cols):
            if core == 0:
                chip = (unit, at16 % 4, at16 // 4)
            else:
                chip = (at16 // 4, at16 % 4, unit)
            x, y, z = chip
            return land_ref[x * 16 + y * 4 + z, :, cols].astype(F32)

        for row in range(8):
            tiles_ref[row * 48 : (row + 1) * 48, :] = jnp.concatenate(
                [
                    unit_shard(unit, row * 2 + half, slice(D, 896))[:, :96]
                    for unit in range(4)
                    for half in range(2)
                ],
                axis=1,
            )
        rows = pl.ds(core * 384, 384)
        copies = [pltpu.make_async_copy(tiles_ref, out_ref.at[rows, :], out_sems.at[4])]
        copies[0].start()
        for at16 in range(16):
            vector_ref[at16] = sum(unit_shard(unit, at16, slice(D, 896)) for unit in range(4))
        for i in range(4, 8):
            take(i).wait()
        for x in range(4):
            for z in range(4):
                for yl in range(2):
                    halves = [
                        land_heads_ref[(x - me_ref[0]) & 3, (yh * 2 + yl) * 4 + z].astype(F32)
                        for yh in range(2)
                    ]
                    at = slice(((x * 4 + z) * 2 + yl) * 24, ((x * 4 + z) * 2 + yl + 1) * 24)
                    for kind in range(3):
                        cols = slice(kind * 192, (kind + 1) * 192)
                        heads_ref[kind, at, :] = jnp.concatenate(
                            [half[:, cols] for half in halves], axis=1
                        )
                    sums_ref[at, :] = halves[0][:, 576:] + halves[1][:, 576:]
        cols = pl.ds(core * 384, 384)
        for kind, target in enumerate((key_ref, value_ref, query_ref)):
            copies.append(
                pltpu.make_async_copy(
                    heads_ref.at[kind], target.at[:, cols], out_sems.at[5 + kind]
                )
            )
            copies[-1].start()
        for k3 in range(4):
            held = stage_ref.at[k3]
            pltpu.make_async_copy(held, held, out_sems.at[k3]).wait()
        for copy in copies:
            copy.wait()

    for core in range(2):
        pl.when((me_ref[3] + other & 1) == core)(functools.partial(emit, core))


def place(me, pieces, before=None):
    before = () if before is None else tuple(before[:6])
    return pl.pallas_call(
        functools.partial(place_kernel, 1 if before else 0),
        out_shape=(
            jax.ShapeDtypeStruct((D, FF), F32),
            jax.ShapeDtypeStruct((FF, D), F32),
        )
        + (jax.ShapeDtypeStruct((D, D), F32),) * 4
        + (jax.ShapeDtypeStruct((D, HEAD), F32), jax.ShapeDtypeStruct((16, 48, 128), F32)),
        in_specs=[SMEM_SPEC]
        + [ANY_SPEC] * 5
        + [ANY_SPEC] * len(before),
        out_specs=(ANY_SPEC,) * 6 + (VMEM_SPEC,) * 2,
        scratch_shapes=[
            pltpu.VMEM((64, 48, 896), BF16),
            pltpu.VMEM((4, 16, 24, 640), BF16),
            pltpu.VMEM((4, 16, 48, D), F32),
            pltpu.VMEM((384, D), F32),
            pltpu.VMEM((3, D, 384), F32),
            pltpu.SemaphoreType.DMA((8,)),
            pltpu.SemaphoreType.DMA((8,)),
        ],
        input_output_aliases={6 + i: i for i in range(6)} if before else {},
        compiler_params=pltpu.CompilerParams(vmem_limit_bytes=40 * 2**20),
        cost_estimate=pl.CostEstimate(flops=0, bytes_accessed=20 * 2**20, transcendentals=0),
    )(me, *pieces, *before)


def embed_kernel(
    count_ref, rows_ref, ids_ref, tokens_ref, gain_ref, bias_ref, wk_hbm, wv_hbm, wq_hbm,
    chunk_ref, normed_ref, routed_ref, w_ref, sems,
):
    for i, w in enumerate((wk_hbm, wv_hbm, wq_hbm)):
        pltpu.make_async_copy(w, w_ref.at[i], sems.at[i]).start()
    places = lax.broadcasted_iota(jnp.int32, (TOK, SLOTS), 0)
    picks = (rows_ref[...] == places).astype(F32).astype(BF16)
    routed = mm_tn(picks, tokens_ref[...])
    gain = gain_ref[...].reshape(1, D)
    bias = bias_ref[...].reshape(1, D)
    normed = layer_norm(routed, gain, bias)[0].astype(BF16)
    routed_ref[...] = routed
    normed_ref[...] = normed
    ids = ids_ref[...]
    halves = jnp.concatenate([ids >> 8, ids & 255] + [jnp.zeros((6, TOK), jnp.int32)], axis=0)
    halves = halves.astype(F32).astype(BF16)
    ids_rows = mm(halves, picks)
    ids_cols = dot(picks, halves, ((0,), (1,)))
    ids_row = ids_rows[0:1] * 256.0 + ids_rows[1:2]
    ids_col = ids_cols[:, 0:1] * 256.0 + ids_cols[:, 1:2]
    slot_row = lax.broadcasted_iota(jnp.int32, (SLOTS, SLOTS), 1)
    slot_col = lax.broadcasted_iota(jnp.int32, (SLOTS, SLOTS), 0)
    count = count_ref[0]
    same = (ids_row == ids_col) & (slot_row < count) & (slot_col < count) | (slot_row == slot_col)
    first = jnp.min(
        jnp.where(same, slot_row.astype(F32), float(SLOTS)), axis=1, keepdims=True
    )
    lanes = lax.broadcasted_iota(jnp.int32, (SLOTS, HEAD), 1)
    slots = lax.broadcasted_iota(jnp.int32, (SLOTS, HEAD), 0)
    is_long = (ids_col == 0.0) & (slots < count)
    marks = jnp.where(lanes == 0, first + 1.0, jnp.where(lanes == 1, count_ref[1] + 1.0, 0.0))
    marks = jnp.where(is_long, 0.0, marks).astype(BF16)
    parts = []
    for i in range(3):
        pltpu.make_async_copy((wk_hbm, wv_hbm, wq_hbm)[i], w_ref.at[i], sems.at[i]).wait()
        parts.append(mm(normed, w_ref[i]).astype(BF16))
    for head in range(HEADS):
        cols = slice(head * HEAD, (head + 1) * HEAD)
        chunk = jnp.concatenate([part[:, cols] for part in parts] + [marks], axis=1)
        for x in range(4):
            chunk_ref[x, HOLDERS[head]] = chunk
    for x in range(4):
        for holder in IDLE:
            chunk_ref[x, holder] = jnp.zeros((SLOTS, 4 * HEAD), BF16)


def embed(scalars, rows, ids, tokens, gain, bias, wk, wv, wq):
    return pl.pallas_call(
        embed_kernel,
        out_shape=(
            jax.ShapeDtypeStruct((4, 16, SLOTS, 4 * HEAD), BF16),
            jax.ShapeDtypeStruct((SLOTS, D), BF16),
            jax.ShapeDtypeStruct((SLOTS, D), F32),
        ),
        in_specs=[SMEM_SPEC] + [VMEM_SPEC] * 5 + [HBM_SPEC] * 3,
        out_specs=(VMEM_SPEC,) * 3,
        scratch_shapes=[pltpu.VMEM((3, D, D), BF16), pltpu.SemaphoreType.DMA((3,))],
        compiler_params=pltpu.CompilerParams(vmem_limit_bytes=58 * 2**20),
        cost_estimate=pl.CostEstimate(
            flops=6 * SLOTS * D * D, bytes_accessed=6 * 2**20, transcendentals=0
        ),
    )(scalars, rows, ids, tokens, gain, bias, wk, wv, wq)


def code_rows(recv_ref, codes_ref):
    lane = lax.broadcasted_iota(jnp.int32, (8, HEAD), 1)
    pick = jnp.where(lane == 0, 1.0, jnp.where(lane == 1, 64.0, 0.0)).astype(BF16)
    for kb in range(8):
        codes = mm_nt(pick, recv_ref[kb % 4, kb // 4, :, 3 * HEAD :])
        row = lax.broadcasted_iota(jnp.int32, (8, RUN), 0)
        codes_ref[kb] = jnp.where((row == 1) & (codes > 0.0), -1.0, codes)


def code_cols(block):
    marks = block[:, 3 * HEAD :].astype(F32)
    return marks[:, 0:1] + 64.0 * marks[:, 1:2]


def attend_kernel(x_ref, recv_ref, out_ref, low_ref, lse_ref, codes_ref):
    x = x_ref[0]
    code_rows(recv_ref, codes_ref)
    for run in range(2):
        q = recv_ref[x, run][:, 2 * HEAD : 3 * HEAD] * SCALE
        last = 4 * run + x
        qcodes = codes_ref[last]

        def block(kb, carry, diagonal):
            peak, total, acc = carry
            kv = recv_ref[lax.rem(kb, 4), kb // 4]
            kcode = code_cols(kv)
            scores = mm_nt(kv[:, :HEAD], q)
            if diagonal:
                rows = lax.broadcasted_iota(jnp.int32, (RUN, RUN), 0)
                cols = lax.broadcasted_iota(jnp.int32, (RUN, RUN), 1)
                allowed = (kcode == qcodes[0:1]) & (rows <= cols)
            else:
                allowed = kcode == qcodes[1:2]
            scores = jnp.where(allowed, scores, NEG_LARGE)
            new_peak = jnp.maximum(peak, jnp.max(scores, axis=0, keepdims=True))
            probs = jnp.exp(scores - new_peak)
            decay = jnp.exp(peak - new_peak)
            total = total * decay + jnp.sum(probs, axis=0, keepdims=True)
            acc = acc * decay + mm_tn(kv[:, HEAD : 2 * HEAD], probs.astype(BF16))
            return new_peak, total, acc

        start = (
            jnp.full((1, RUN), NEG_LARGE, F32),
            jnp.zeros((1, RUN), F32),
            jnp.zeros((HEAD, RUN), F32),
        )
        carry = block(last, start, True)
        peak, total, acc = lax.fori_loop(
            0, last, lambda kb, carry: block(kb, carry, False), carry
        )
        mixed = (acc / total).T
        out_ref[run] = mixed
        low_ref[run, :, :HEAD] = mixed.astype(BF16)
        low_ref[run, :, HEAD:] = jnp.zeros((RUN, HEAD), BF16)
        lse_ref[run] = peak + jnp.log(total)


def attend(x, recv):
    return pl.pallas_call(
        attend_kernel,
        out_shape=(
            jax.ShapeDtypeStruct((2, RUN, HEAD), F32),
            jax.ShapeDtypeStruct((2, RUN, 2 * HEAD), BF16),
            jax.ShapeDtypeStruct((2, 1, RUN), F32),
        ),
        in_specs=[SMEM_SPEC, VMEM_SPEC],
        out_specs=(VMEM_SPEC,) * 3,
        scratch_shapes=[pltpu.VMEM((8, 8, RUN), F32)],
        compiler_params=pltpu.CompilerParams(vmem_limit_bytes=14 * 2**20),
        cost_estimate=pl.CostEstimate(
            flops=24 * 768 * 3072 * 64, bytes_accessed=3 * 2**20, transcendentals=768 * 3072
        ),
    )(x, recv)


def attend_back_kernel(
    x_ref, recv_ref, do_ref, mixed_ref, lse_ref, dq_ref, dkv_ref, codes_ref, acc_ref
):
    x = x_ref[0]
    acc_ref[...] = jnp.zeros_like(acc_ref)
    code_rows(recv_ref, codes_ref)
    for run in range(2):
        q = recv_ref[x, run][:, 2 * HEAD : 3 * HEAD] * SCALE
        do = do_ref[run][:, :HEAD]
        last = 4 * run + x
        qcodes = codes_ref[last]
        lse = lse_ref[run]
        inner = dot(
            jnp.ones((8, HEAD), F32), do.astype(F32) * mixed_ref[run], ((1,), (1,)), EXACT
        )[0:1]

        def block(kb, dq, diagonal):
            kv = recv_ref[lax.rem(kb, 4), kb // 4]
            keys = kv[:, :HEAD]
            kcode = code_cols(kv)
            scores = mm_nt(keys, q)
            if diagonal:
                rows = lax.broadcasted_iota(jnp.int32, (RUN, RUN), 0)
                cols = lax.broadcasted_iota(jnp.int32, (RUN, RUN), 1)
                allowed = (kcode == qcodes[0:1]) & (rows <= cols)
            else:
                allowed = kcode == qcodes[1:2]
            probs = jnp.where(allowed, jnp.exp(scores - lse), 0.0)
            grad_probs = mm_nt(kv[:, HEAD : 2 * HEAD], do)
            grad_raw = (probs * (grad_probs - inner)).astype(BF16)
            dk = mm(grad_raw, q)
            dv = mm(probs.astype(BF16), do)
            acc_ref[kb] += jnp.concatenate([dk, dv], axis=1)
            return dq + mm_tn(keys, grad_raw)

        dq = block(last, jnp.zeros((HEAD, RUN), F32), True)
        dq = lax.fori_loop(0, last, lambda kb, carry: block(kb, carry, False), dq)
        dq_ref[run] = (dq * SCALE).T.astype(BF16)
    for kb in range(8):
        dkv_ref[kb % 4, kb // 4] = acc_ref[kb].astype(BF16)


def attend_back(x, recv, do, mixed, lse):
    return pl.pallas_call(
        attend_back_kernel,
        out_shape=(
            jax.ShapeDtypeStruct((2, RUN, HEAD), BF16),
            jax.ShapeDtypeStruct((4, 2, RUN, 2 * HEAD), BF16),
        ),
        in_specs=[SMEM_SPEC] + [VMEM_SPEC] * 4,
        out_specs=(VMEM_SPEC,) * 2,
        scratch_shapes=[pltpu.VMEM((8, 8, RUN), F32), pltpu.VMEM((8, RUN, 2 * HEAD), F32)],
        compiler_params=pltpu.CompilerParams(vmem_limit_bytes=18 * 2**20),
        cost_estimate=pl.CostEstimate(
            flops=60 * 768 * 3072 * 64, bytes_accessed=6 * 2**20, transcendentals=768 * 3072
        ),
    )(x, recv, do, mixed, lse)


ROOT = 0.7978845608028654
CUBE = 0.044715


def feed_kernel(
    parts_ref, routed_ref, gate_ref, branch_ref, low_ref, grad_act_ref, gain_ref, bias_ref,
    core_ref, wo_hbm, we_hbm,
    kept_ref, given_ref, back_ref, projected_ref, hidden_ref, logit_ref, vector_ref, act_ref,
    wo_ref, we_ref, sems,
):
    copies = [pltpu.make_async_copy(wo_hbm, wo_ref, sems.at[4])]
    for i in range(4):
        cols = pl.ds(i * D, D)
        copies.append(pltpu.make_async_copy(we_hbm.at[:, cols], we_ref.at[i], sems.at[i]))
    for copy in copies:
        copy.start()
    mixed = jnp.concatenate([parts_ref[holder, :, :HEAD] for holder in HOLDERS], axis=1)
    copies[0].wait()
    projected = mm(mixed, wo_ref[...])
    projected_ref[...] = projected
    routed = routed_ref[...]
    gain = gain_ref[...]
    normed, unit, inv = layer_norm(routed + projected, gain, bias_ref[...])
    normed = normed.astype(BF16)
    grad_branch = branch_ref[...]
    grad_contracted = low_ref[...]
    grad_normed = jnp.zeros((SLOTS, D), F32)
    inner = jnp.sum(grad_branch * projected, axis=1, keepdims=True)
    for i in range(4):
        copies[i + 1].wait()
        v = mm(normed, we_ref[i])
        t = jnp.tanh(ROOT * (v + CUBE * v * v * v))
        half = 0.5 * (1.0 + t)
        act = v * half
        slope = half + 0.5 * v * (1.0 - t * t) * (ROOT * (1.0 + 3.0 * CUBE * v * v))
        grad_act = grad_act_ref[:, i * D : (i + 1) * D]
        inner += jnp.sum(act * grad_act, axis=1, keepdims=True)
        act = act.astype(BF16)
        grad_expanded = (grad_act * slope).astype(BF16)
        grad_normed += mm_nt(grad_expanded, we_ref[i])
        act_ref[:, i * D : (i + 1) * D] = act

        @pl.when(core_ref[0] == 0)
        def _(i=i, grad_expanded=grad_expanded, act=act):
            kept_ref[i, :, :D] = normed
            kept_ref[i, :, D : 2 * D] = grad_expanded
            given_ref[i, :, :D] = act
            given_ref[i, :, D : 2 * D] = grad_contracted

        @pl.when(core_ref[0] == 1)
        def _(i=i, grad_expanded=grad_expanded, act=act):
            given_ref[i, :, :D] = normed
            given_ref[i, :, D : 2 * D] = grad_expanded
            kept_ref[i, :, :D] = act
            kept_ref[i, :, D : 2 * D] = grad_contracted
    grad_logit = (1.0 - gate_ref[...]) * inner
    logit_ref[...] = grad_logit
    grad_hidden = layer_norm_back(grad_normed, unit, inv, gain)
    hidden_ref[...] = grad_hidden
    grad_projected = (grad_branch + grad_hidden).astype(BF16)
    grad_mixed = mm_nt(grad_projected, wo_ref[...]).astype(BF16)
    for head in range(HEADS):
        back_ref[HOLDERS[head], :, :HEAD] = grad_mixed[:, head * HEAD : (head + 1) * HEAD]
        back_ref[HOLDERS[head], :, HEAD:] = jnp.zeros((SLOTS, HEAD), BF16)
    for holder in IDLE:
        back_ref[holder] = jnp.zeros((SLOTS, 2 * HEAD), BF16)
    halves = (mixed[:, :384], mixed[:, 384:])
    for i in range(4):
        part = grad_projected[:, i * 192 : (i + 1) * 192]
        kept_ref[i, :, 2 * D + 384 :] = part
        given_ref[i, :, 2 * D + 384 :] = part
    for core in range(2):

        @pl.when(core_ref[0] == core)
        def _(core=core):
            for i in range(4):
                kept_ref[i, :, 2 * D : 2 * D + 384] = halves[core]
                given_ref[i, :, 2 * D : 2 * D + 384] = halves[1 - core]

    vector_ref[0:1] = jnp.sum(grad_logit * routed, axis=0, keepdims=True)
    vector_ref[1:2] = jnp.sum(grad_normed * unit, axis=0, keepdims=True)
    vector_ref[2:3] = jnp.sum(grad_normed, axis=0, keepdims=True)


def feed(parts, routed, gate, branch, low, grad_act, gain, bias, core, wo, we):
    return pl.pallas_call(
        feed_kernel,
        out_shape=(
            jax.ShapeDtypeStruct((4, SLOTS, 2 * D + 576), BF16),
            jax.ShapeDtypeStruct((4, SLOTS, 2 * D + 576), BF16),
            jax.ShapeDtypeStruct((16, SLOTS, 2 * HEAD), BF16),
            jax.ShapeDtypeStruct((SLOTS, D), F32),
            jax.ShapeDtypeStruct((SLOTS, D), F32),
            jax.ShapeDtypeStruct((SLOTS, 1), F32),
            jax.ShapeDtypeStruct((3, D), F32),
            jax.ShapeDtypeStruct((SLOTS, FF), BF16),
        ),
        in_specs=[VMEM_SPEC] * 8 + [SMEM_SPEC] + [HBM_SPEC] * 2,
        out_specs=(VMEM_SPEC,) * 8,
        scratch_shapes=[
            pltpu.VMEM((D, D), BF16),
            pltpu.VMEM((4, D, D), BF16),
            pltpu.SemaphoreType.DMA((5,)),
        ],
        compiler_params=pltpu.CompilerParams(vmem_limit_bytes=58 * 2**20),
        cost_estimate=pl.CostEstimate(
            flops=20 * SLOTS * D * D, bytes_accessed=10 * 2**20, transcendentals=SLOTS * FF
        ),
    )(parts, routed, gate, branch, low, grad_act, gain, bias, core, wo, we)


def unit_kernel(*refs):
    parts, (vector_ref, out_ref) = refs[:4], refs[4:]

    def outer(left, right):
        total = jnp.zeros((left.stop - left.start, right.stop - right.start), F32)
        for part in parts:
            total += mm_tn(part[:, left], part[:, right])
        return total.astype(BF16)

    tile = outer(slice(2 * D, 2 * D + 384), slice(2 * D + 384, 2 * D + 576))
    for block in range(2):
        unit = outer(slice(block * 384, (block + 1) * 384), slice(D, 2 * D))
        for i in range(8):
            at = block * 8 + i
            out_ref[at // 4, at % 4, :, :D] = unit[i * 48 : (i + 1) * 48]
            out_ref[at // 4, at % 4, :, D:] = jnp.concatenate(
                [
                    tile[(at // 2) * 48 : (at // 2 + 1) * 48, (at % 2) * 96 : (at % 2 + 1) * 96],
                    vector_ref[at],
                ],
                axis=1,
            )


def unit_grads(parts, vectors):
    return pl.pallas_call(
        unit_kernel,
        out_shape=jax.ShapeDtypeStruct((4, 4, 48, 896), BF16),
        in_specs=[VMEM_SPEC] * 5,
        out_specs=VMEM_SPEC,
        compiler_params=pltpu.CompilerParams(vmem_limit_bytes=14 * 2**20),
        cost_estimate=pl.CostEstimate(
            flops=2 * 384 * D * D, bytes_accessed=3 * 2**20, transcendentals=0
        ),
    )(*parts, vectors)


def embed_back_kernel(
    back_ref, routed_ref, hidden_ref, logit_ref, rows_ref, grad_ref, router_ref, gain_ref,
    wk_hbm, wv_hbm, wq_hbm, out_ref, w_ref, sems,
):
    copies = [
        pltpu.make_async_copy(w, w_ref.at[i], sems.at[i])
        for i, w in enumerate((wk_hbm, wv_hbm, wq_hbm))
    ]
    for copy in copies:
        copy.start()
    routed = routed_ref[...]
    gain = gain_ref[...].reshape(1, D)
    unused, unit, inv = layer_norm(routed, gain, 0.0)
    grad_normed = jnp.zeros((SLOTS, D), F32)
    for i in range(3):
        grads = jnp.concatenate(
            [back_ref[holder, :, i * HEAD : (i + 1) * HEAD] for holder in HOLDERS], axis=1
        )
        copies[i].wait()
        grad_normed += mm_nt(grads, w_ref[i])
    grad_rows = (
        logit_ref[...] * router_ref[...].reshape(1, D)
        + hidden_ref[...]
        + layer_norm_back(grad_normed, unit, inv, gain)
    )
    places = lax.broadcasted_iota(jnp.int32, (TOK, SLOTS), 0)
    picks = (rows_ref[...] == places).astype(F32)
    out_ref[...] = (
        grad_ref[...].astype(F32) + dot(picks, grad_rows, ((1,), (0,)), EXACT)
    ).astype(BF16)


def embed_back(back, routed, hidden, logit, rows, grad, router, gain, wk, wv, wq):
    return pl.pallas_call(
        embed_back_kernel,
        out_shape=jax.ShapeDtypeStruct((TOK, D), BF16),
        in_specs=[VMEM_SPEC] * 8 + [HBM_SPEC] * 3,
        out_specs=VMEM_SPEC,
        scratch_shapes=[pltpu.VMEM((3, D, D), BF16), pltpu.SemaphoreType.DMA((3,))],
        compiler_params=pltpu.CompilerParams(vmem_limit_bytes=58 * 2**20),
        cost_estimate=pl.CostEstimate(
            flops=6 * SLOTS * D * D, bytes_accessed=6 * 2**20, transcendentals=0
        ),
    )(back, routed, hidden, logit, rows, grad, router, gain, wk, wv, wq)


def body(
    tokens,
    router,
    gain_one,
    bias_one,
    w_query,
    w_key,
    w_value,
    w_out,
    gain_two,
    bias_two,
    w_expand,
    w_contract,
    cotangent,
    seq_ids,
    routed_rows,
    routed_count,
):
    x_at = lax.axis_index("x").astype(jnp.int32)
    core_at = lax.axis_index("c").astype(jnp.int32)
    y_at = lax.axis_index(("yh", "yl")).astype(jnp.int32)
    z_at = lax.axis_index("z").astype(jnp.int32)
    first_at = jnp.where(core_at == 0, x_at, z_at)
    second_at = jnp.where(core_at == 0, z_at, x_at)
    row_index = routed_rows[0, 0]
    routed_total = routed_count[0, 0]
    x_local = tokens[0]
    place_at = lax.axis_index(("z", "c")).astype(jnp.int32)
    to_heads, normed_low, routed_x = embed(
        jnp.stack([routed_total, place_at]),
        routed_rows[0],
        seq_ids,
        x_local,
        gain_one,
        bias_one,
        w_key,
        w_value,
        w_query,
    )
    recv = swap(to_heads.reshape(64, SLOTS, 4 * HEAD), ("x",) + SIXTEEN)
    w_part = jnp.concatenate(
        [
            lax.dynamic_slice(
                w,
                (lax.axis_index(("x", "z", "yl")) * 24, (core_at * 2 + lax.axis_index("yh")) * 3 * HEAD),
                (24, 3 * HEAD),
            )
            for w in (w_key, w_value, w_query)
        ],
        axis=1,
    ).astype(F32)
    recv, w_part = lax.optimization_barrier((recv, w_part))
    recv = recv.reshape(4, 2, RUN, 4 * HEAD)
    normed_block = lax.all_gather(normed_low, SIXTEEN, axis=0, tiled=True)

    is_valid = jnp.arange(SLOTS, dtype=jnp.int32) < routed_total
    picks = row_index[:, None] == jnp.arange(TOK, dtype=jnp.int32)[None, :]
    pick_low = picks.astype(BF16)
    pick_full = picks.astype(F32)
    gate_value = jax.nn.sigmoid(jnp.sum(routed_x * router[None, :], axis=-1))
    gate_used = jnp.where(is_valid, gate_value, 0.0)
    grad_local = cotangent[0]
    grad_branch = gate_used[:, None] * mm(pick_low, grad_local)
    grad_contracted = grad_branch.astype(BF16)
    grad_activated = mm_nt(grad_contracted, w_contract)

    mixed_here, mixed_low, lse = attend(x_at[None], recv)
    mixed_parts = swap(mixed_low.reshape(16, SLOTS, 2 * HEAD), SIXTEEN)
    (kept, given, do_parts, projected, grad_hidden, grad_logit, vectors, activated_low) = feed(
        mixed_parts,
        routed_x,
        gate_value[:, None],
        grad_branch,
        grad_contracted,
        grad_activated,
        gain_two[None],
        bias_two[None],
        core_at[None],
        w_out,
        w_expand,
    )
    given = lax.ppermute(given, "c", [(0, 1), (1, 0)])
    eight = jnp.concatenate([kept, given], axis=1)
    eight = ring_swap(eight, first_at, lambda step: ring_pairs(0, step), CUBE_AXES)
    do_parts = swap(do_parts, SIXTEEN)
    eight, do_parts, normed_block = lax.optimization_barrier((eight, do_parts, normed_block))
    vectors = jnp.pad(vectors.astype(BF16).reshape(16, 48, 3), ((0, 0), (0, 0), (0, 29)))
    partial_grads = unit_grads(eight, vectors)
    do_parts, partial_grads = lax.optimization_barrier((do_parts, partial_grads))
    grad_q, grad_kv = attend_back(
        x_at[None], recv, do_parts.reshape(2, RUN, 2 * HEAD), mixed_here, lse
    )
    partial_grads = ring_swap(
        partial_grads, second_at, lambda step: ring_pairs(1, step), CUBE_AXES
    )
    partial_grads, grad_kv = lax.optimization_barrier((partial_grads, grad_kv))
    partial_grads = sum(part.astype(F32) for part in partial_grads).astype(BF16)
    partial_grads = ring_swap(
        partial_grads,
        y_at,
        lambda step: [(i, (i + step) % 4) for i in range(4)],
        ("yh", "yl"),
    )
    own_grads = sum(part.astype(F32) for part in partial_grads).astype(BF16)
    grad_kv, own_grads = lax.optimization_barrier((grad_kv, own_grads))
    grad_kv = swap(grad_kv, ("x",))
    grad_kv_sum = jnp.sum(grad_kv.astype(F32), axis=0).astype(BF16)
    grad_heads = jnp.concatenate(
        [grad_kv_sum.reshape(2 * RUN, 2 * HEAD), grad_q.reshape(2 * RUN, HEAD)], axis=1
    )
    units = lax.all_gather(own_grads, CHIPS, axis=0, tiled=False)
    branch = projected + mm(activated_low, w_contract)
    output = (
        x_local.astype(F32)
        + dot(pick_full, gate_used[:, None] * branch, ((0,), (0,)), EXACT)
    ).astype(BF16)

    grad_qkv = mm_tn(normed_block, grad_heads).astype(BF16).reshape(32, 24, 3 * HEAD)
    column_sum = jnp.sum(grad_heads.astype(F32), axis=0).astype(BF16)
    column_sum = jnp.broadcast_to(column_sum[None, None, :], (32, 8, 3 * HEAD))
    grad_qkv = swap(jnp.concatenate([grad_qkv, column_sum], axis=1), ("x", "z", "yl"))
    grad_qkv, output = lax.optimization_barrier((grad_qkv, output))
    grad_qkv = jnp.sum(grad_qkv.reshape(4, 4, 2, 32, 3 * HEAD)[:, :3].astype(F32), axis=(0, 2))
    grad_qkv = jnp.concatenate(
        [
            grad_qkv[:, :, kind * HEAD : (kind + 1) * HEAD].transpose(1, 0, 2).reshape(32, 3 * HEAD)
            for kind in range(3)
        ],
        axis=1,
    )
    column_sum = grad_qkv[24]
    grad_qkv = grad_qkv[:24]
    norm_sums = jnp.stack(
        [jnp.sum(w_part * grad_qkv, axis=1), jnp.sum(w_part * column_sum[None, :], axis=1)], axis=1
    )
    own_qkv = jnp.concatenate([grad_qkv, jnp.pad(norm_sums, ((0, 0), (0, 62)))], axis=1)
    own_qkv = own_qkv.astype(BF16)
    heads = spread(own_qkv, ("yh", "yl", "z"))
    heads, grad_heads = lax.optimization_barrier((heads, grad_heads))
    heads = [heads] + [
        lax.ppermute(heads, "x", [((i + step) % 4, i) for i in range(4)]) for step in (1, 2, 3)
    ]
    back = swap(
        jnp.pad(grad_heads, ((0, 0), (0, HEAD))).reshape(16, SLOTS, 4 * HEAD), SIXTEEN
    )
    input_grad = embed_back(
        back,
        routed_x,
        grad_hidden,
        grad_logit,
        routed_rows[0],
        grad_local,
        router,
        gain_one,
        w_key,
        w_value,
        w_query,
    )
    heads, input_grad = lax.optimization_barrier((heads, input_grad))
    heads = heads + other_core(heads)
    units, heads = lax.optimization_barrier((units, heads))
    me = jnp.stack([x_at, y_at, z_at, core_at])
    first = place(me, [units] + heads[:4])
    placed = place(me, other_core([units]) + heads[4:], first)
    final_expand, final_contract, final_out, final_key, final_value, final_query = placed[:6]
    norm_sums = (first[6][:, :2] + placed[6][:, :2]).T
    grad_gain_one = (norm_sums[0] - bias_one * norm_sums[1]) / gain_one
    grad_bias_one = norm_sums[1]
    vectors = first[7][:, :, 96:] + placed[7][:, :, 96:]
    vectors = vectors[:, :, :3].reshape(3, D)
    return (
        output[None],
        input_grad[None],
        vectors[0],
        grad_gain_one,
        grad_bias_one,
        final_query,
        final_key,
        final_value,
        final_out,
        vectors[1],
        vectors[2],
        final_expand,
        final_contract,
    )


def solution(mesh):
    fine = Mesh(mesh.devices.reshape(2, 4, 4, 2, 2), ("yh", "x", "z", "c", "yl"))
    seq = ("yh", "x", "z", "c")
    in_specs = (
        (P("yl", seq, None),)
        + (P(),) * 11
        + (P("yl", seq, None), P("yl", seq), P("yl", seq, None), P("yl", seq))
    )
    out_specs = (P("yl", seq, None),) * 2 + (P(),) * 11
    return jax.shard_map(body, mesh=fine, in_specs=in_specs, out_specs=out_specs, check_vma=False)
```

```python
import functools

import jax
import jax.numpy as jnp
from jax import lax
from jax.experimental import pallas as pl
from jax.experimental.pallas import tpu as pltpu
from jax.sharding import Mesh
from jax.sharding import PartitionSpec as P

HEAD = 64
HEADS = 12
SLOTS = 48
D = 768
FF = 3072
TOK = 256
RUN = 384
EPSILON = 1e-05
NEG_LARGE = -1e30
EXACT = lax.Precision.HIGHEST
SCALE = float(HEAD) ** (-0.5)
F32 = jnp.float32
BF16 = jnp.bfloat16

SIXTEEN = ("yh", "z", "c")
HOLDERS = [yh * 8 + z * 2 + c for c in range(2) for yh in range(2) for z in range(3)]
IDLE = [yh * 8 + 6 + c for yh in range(2) for c in range(2)]
SIZES = {"yh": 2, "x": 4, "z": 4, "c": 2, "yl": 2}


def width_of(axes):
    total = 1
    for axis in axes:
        total *= SIZES[axis]
    return total


def swap(parts, axes):
    return lax.all_to_all(parts, axes, split_axis=0, concat_axis=0, tiled=True)


def spread(part, axes):
    parts = width_of(axes)
    return swap(jnp.broadcast_to(part[None], (parts,) + part.shape), axes)


CHIPS = ("x", "yh", "yl", "z")
SMEM_SPEC = pl.BlockSpec(memory_space=pltpu.SMEM)
ANY_SPEC = pl.BlockSpec(memory_space=pl.ANY)
VMEM_SPEC = pl.BlockSpec(memory_space=pltpu.VMEM)
HBM_SPEC = pl.BlockSpec(memory_space=pltpu.HBM)


CUBE_AXES = ("x", "z", "c")
FIRST = (("x", "z"), ("z", "x"))


def ring_pairs(turn, step):
    pairs = []
    for x in range(4):
        for z in range(4):
            for c in range(2):
                to = {"x": x, "z": z}
                axis = FIRST[c][turn]
                to[axis] = (to[axis] + step) % 4
                pairs.append((x * 8 + z * 2 + c, to["x"] * 8 + to["z"] * 2 + c))
    return pairs


def ring_swap(parts, at, pairs_of, axes):
    mine = [lax.dynamic_index_in_dim(parts, at, 0, keepdims=False)]
    for step in (1, 2, 3):
        part = lax.dynamic_index_in_dim(parts, lax.rem(at + step, 4), 0, keepdims=False)
        mine.append(lax.ppermute(part, axes, pairs_of(step)))
    return mine


def other_core(pieces):
    return [lax.ppermute(piece, "c", [(0, 1), (1, 0)]) for piece in pieces]


def dot(left, right, dims, precision=None):
    return lax.dot_general(
        left, right, (dims, ((), ())), precision=precision, preferred_element_type=F32
    )


def mm(left, right):
    return dot(left, right, ((1,), (0,)))


def mm_tn(left, right):
    return dot(left, right, ((0,), (0,)))


def mm_nt(left, right):
    return dot(left, right, ((1,), (1,)))


def layer_norm(values_in, gain_vec, bias_vec):
    center = values_in - jnp.mean(values_in, axis=-1, keepdims=True)
    spread_ = jnp.mean(center * center, axis=-1, keepdims=True)
    inv = lax.rsqrt(spread_ + EPSILON)
    unit = center * inv
    return unit * gain_vec + bias_vec, unit, inv


def layer_norm_back(grad, unit, inv, gain_vec):
    scaled = grad * gain_vec
    mean_one = jnp.mean(scaled, axis=-1, keepdims=True)
    mean_two = jnp.mean(scaled * unit, axis=-1, keepdims=True)
    return inv * (scaled - mean_one - unit * mean_two)


def place_kernel(
    other, me_ref, units_in, *refs
):
    if other:
        refs = refs[3:]
    (
        expand_ref, contract_ref, out_ref, vector_ref,
        land_ref, stage_ref, tiles_ref, in_sems, out_sems,
    ) = refs

    def take(x):
        rows = pl.ds(x * 16, 16)
        return pltpu.make_async_copy(units_in.at[rows], land_ref.at[rows], in_sems.at[x])

    for x in range(4):
        take(x).start()

    def emit(core):
        for x in range(4):
            take(x).wait()
            for y in range(4):
                for z in range(4):
                    staged = stage_ref.at[x, y * 4 + z]
                    staged[...] = land_ref[x * 16 + y * 4 + z, :, :D].astype(F32)
                    if core == 0:
                        target = expand_ref.at[pl.ds((z * 4 + y) * 48, 48), pl.ds(x * D, D)]
                    else:
                        target = contract_ref.at[pl.ds(z * D + (x * 4 + y) * 48, 48), :]
                    pltpu.make_async_copy(staged, target, out_sems.at[x]).start()

        def unit_shard(unit, at16):
            if core == 0:
                x, y, z = unit, at16 % 4, at16 // 4
            else:
                x, y, z = at16 // 4, at16 % 4, unit
            return land_ref[x * 16 + y * 4 + z, :, D:].astype(F32)

        for row in range(8):
            tiles_ref[row * 48 : (row + 1) * 48, :] = jnp.concatenate(
                [
                    unit_shard(unit, row * 2 + half)[:, :96]
                    for unit in range(4)
                    for half in range(2)
                ],
                axis=1,
            )
        copy = pltpu.make_async_copy(
            tiles_ref, out_ref.at[pl.ds(core * 384, 384), :], out_sems.at[4]
        )
        copy.start()
        for at16 in range(16):
            vector_ref[at16] = sum(unit_shard(unit, at16)[:, 96:] for unit in range(4))
        for x in range(4):
            held = stage_ref.at[x]
            pltpu.make_async_copy(held, held, out_sems.at[x]).wait()
        copy.wait()

    for core in range(2):
        pl.when((me_ref[3] + other & 1) == core)(functools.partial(emit, core))


def place(me, units, before=None):
    before = () if before is None else tuple(before[:3])
    return pl.pallas_call(
        functools.partial(place_kernel, 1 if before else 0),
        out_shape=(
            jax.ShapeDtypeStruct((D, FF), F32),
            jax.ShapeDtypeStruct((FF, D), F32),
            jax.ShapeDtypeStruct((D, D), F32),
            jax.ShapeDtypeStruct((16, 48, 32), F32),
        ),
        in_specs=[SMEM_SPEC, ANY_SPEC] + [ANY_SPEC] * len(before),
        out_specs=(ANY_SPEC,) * 3 + (VMEM_SPEC,),
        scratch_shapes=[
            pltpu.VMEM((64, 48, 896), BF16),
            pltpu.VMEM((4, 16, 48, D), F32),
            pltpu.VMEM((384, D), F32),
            pltpu.SemaphoreType.DMA((4,)),
            pltpu.SemaphoreType.DMA((5,)),
        ],
        input_output_aliases={2 + i: i for i in range(3)} if before else {},
        compiler_params=pltpu.CompilerParams(vmem_limit_bytes=32 * 2**20),
        cost_estimate=pl.CostEstimate(flops=0, bytes_accessed=20 * 2**20, transcendentals=0),
    )(me, units, *before)


def place_heads_kernel(me_ref, own_ref, other_ref, key_ref, value_ref, query_ref, sums_ref):
    def emit(by_core):
        for x in range(4):
            for z in range(4):
                for yl in range(2):
                    blocks = [
                        by_core[c][x * 16 + (yh * 2 + yl) * 4 + z].astype(F32)
                        for c in range(2)
                        for yh in range(2)
                    ]
                    at = ((x * 4 + z) * 2 + yl) * 24
                    for kind, out_ref in enumerate((key_ref, value_ref, query_ref)):
                        out_ref[at : at + 24, :] = jnp.concatenate(
                            [block[:, kind * 192 : (kind + 1) * 192] for block in blocks], axis=1
                        )
                    sums_ref[at : at + 24, :] = sum(block[:, 576:] for block in blocks)

    @pl.when(me_ref[3] == 0)
    def _():
        emit((own_ref, other_ref))

    @pl.when(me_ref[3] == 1)
    def _():
        emit((other_ref, own_ref))


def place_heads(me, own, other):
    return pl.pallas_call(
        place_heads_kernel,
        out_shape=(jax.ShapeDtypeStruct((D, D), F32),) * 3
        + (jax.ShapeDtypeStruct((D, HEAD), F32),),
        in_specs=[SMEM_SPEC] + [VMEM_SPEC] * 2,
        out_specs=(VMEM_SPEC,) * 4,
        compiler_params=pltpu.CompilerParams(vmem_limit_bytes=18 * 2**20),
        cost_estimate=pl.CostEstimate(flops=0, bytes_accessed=12 * 2**20, transcendentals=0),
    )(me, own, other)


def embed_kernel(
    count_ref, rows_ref, ids_ref, tokens_ref, gain_ref, bias_ref, wk_hbm, wv_hbm, wq_hbm,
    chunk_ref, normed_ref, routed_ref, w_ref, sems,
):
    for i, w in enumerate((wk_hbm, wv_hbm, wq_hbm)):
        pltpu.make_async_copy(w, w_ref.at[i], sems.at[i]).start()
    places = lax.broadcasted_iota(jnp.int32, (TOK, SLOTS), 0)
    picks = (rows_ref[...] == places).astype(F32).astype(BF16)
    routed = mm_tn(picks, tokens_ref[...])
    gain = gain_ref[...].reshape(1, D)
    bias = bias_ref[...].reshape(1, D)
    normed = layer_norm(routed, gain, bias)[0].astype(BF16)
    routed_ref[...] = routed
    normed_ref[...] = normed
    ids = ids_ref[...]
    halves = jnp.concatenate([ids >> 8, ids & 255] + [jnp.zeros((6, TOK), jnp.int32)], axis=0)
    halves = halves.astype(F32).astype(BF16)
    ids_rows = mm(halves, picks)
    ids_cols = dot(picks, halves, ((0,), (1,)))
    ids_row = ids_rows[0:1] * 256.0 + ids_rows[1:2]
    ids_col = ids_cols[:, 0:1] * 256.0 + ids_cols[:, 1:2]
    slot_row = lax.broadcasted_iota(jnp.int32, (SLOTS, SLOTS), 1)
    slot_col = lax.broadcasted_iota(jnp.int32, (SLOTS, SLOTS), 0)
    count = count_ref[0]
    same = (ids_row == ids_col) & (slot_row < count) & (slot_col < count) | (slot_row == slot_col)
    first = jnp.min(
        jnp.where(same, slot_row.astype(F32), float(SLOTS)), axis=1, keepdims=True
    )
    lanes = lax.broadcasted_iota(jnp.int32, (SLOTS, HEAD), 1)
    slots = lax.broadcasted_iota(jnp.int32, (SLOTS, HEAD), 0)
    is_long = (ids_col == 0.0) & (slots < count)
    marks = jnp.where(lanes == 0, first + 1.0, jnp.where(lanes == 1, count_ref[1] + 1.0, 0.0))
    marks = jnp.where(is_long, 0.0, marks).astype(BF16)
    parts = []
    for i in range(3):
        pltpu.make_async_copy((wk_hbm, wv_hbm, wq_hbm)[i], w_ref.at[i], sems.at[i]).wait()
        parts.append(mm(normed, w_ref[i]).astype(BF16))
    for head in range(HEADS):
        cols = slice(head * HEAD, (head + 1) * HEAD)
        chunk = jnp.concatenate([part[:, cols] for part in parts] + [marks], axis=1)
        for x in range(4):
            chunk_ref[x, HOLDERS[head]] = chunk
    for x in range(4):
        for holder in IDLE:
            chunk_ref[x, holder] = jnp.zeros((SLOTS, 4 * HEAD), BF16)


def embed(scalars, rows, ids, tokens, gain, bias, wk, wv, wq):
    return pl.pallas_call(
        embed_kernel,
        out_shape=(
            jax.ShapeDtypeStruct((4, 16, SLOTS, 4 * HEAD), BF16),
            jax.ShapeDtypeStruct((SLOTS, D), BF16),
            jax.ShapeDtypeStruct((SLOTS, D), F32),
        ),
        in_specs=[SMEM_SPEC] + [VMEM_SPEC] * 5 + [HBM_SPEC] * 3,
        out_specs=(VMEM_SPEC,) * 3,
        scratch_shapes=[pltpu.VMEM((3, D, D), BF16), pltpu.SemaphoreType.DMA((3,))],
        compiler_params=pltpu.CompilerParams(vmem_limit_bytes=58 * 2**20),
        cost_estimate=pl.CostEstimate(
            flops=6 * SLOTS * D * D, bytes_accessed=6 * 2**20, transcendentals=0
        ),
    )(scalars, rows, ids, tokens, gain, bias, wk, wv, wq)


def code_rows(recv_ref, codes_ref):
    lane = lax.broadcasted_iota(jnp.int32, (8, HEAD), 1)
    pick = jnp.where(lane == 0, 1.0, jnp.where(lane == 1, 64.0, 0.0)).astype(BF16)
    for kb in range(8):
        codes = mm_nt(pick, recv_ref[kb % 4, kb // 4, :, 3 * HEAD :])
        row = lax.broadcasted_iota(jnp.int32, (8, RUN), 0)
        codes_ref[kb] = jnp.where((row == 1) & (codes > 0.0), -1.0, codes)


def code_cols(block):
    marks = block[:, 3 * HEAD :].astype(F32)
    return marks[:, 0:1] + 64.0 * marks[:, 1:2]


def attend_kernel(x_ref, recv_ref, out_ref, low_ref, lse_ref, codes_ref):
    x = x_ref[0]
    code_rows(recv_ref, codes_ref)
    for run in range(2):
        q = recv_ref[x, run][:, 2 * HEAD : 3 * HEAD] * SCALE
        last = 4 * run + x
        qcodes = codes_ref[last]

        def block(kb, carry, diagonal):
            peak, total, acc = carry
            kv = recv_ref[lax.rem(kb, 4), kb // 4]
            kcode = code_cols(kv)
            scores = mm_nt(kv[:, :HEAD], q)
            if diagonal:
                rows = lax.broadcasted_iota(jnp.int32, (RUN, RUN), 0)
                cols = lax.broadcasted_iota(jnp.int32, (RUN, RUN), 1)
                allowed = (kcode == qcodes[0:1]) & (rows <= cols)
            else:
                allowed = kcode == qcodes[1:2]
            scores = jnp.where(allowed, scores, NEG_LARGE)
            new_peak = jnp.maximum(peak, jnp.max(scores, axis=0, keepdims=True))
            probs = jnp.exp(scores - new_peak)
            decay = jnp.exp(peak - new_peak)
            total = total * decay + jnp.sum(probs, axis=0, keepdims=True)
            acc = acc * decay + mm_tn(kv[:, HEAD : 2 * HEAD], probs.astype(BF16))
            return new_peak, total, acc

        start = (
            jnp.full((1, RUN), NEG_LARGE, F32),
            jnp.zeros((1, RUN), F32),
            jnp.zeros((HEAD, RUN), F32),
        )
        carry = block(last, start, True)
        peak, total, acc = lax.fori_loop(
            0, last, lambda kb, carry: block(kb, carry, False), carry
        )
        mixed = (acc / total).T
        out_ref[run] = mixed
        low_ref[run, :, :HEAD] = mixed.astype(BF16)
        low_ref[run, :, HEAD:] = jnp.zeros((RUN, HEAD), BF16)
        lse_ref[run] = peak + jnp.log(total)


def attend(x, recv):
    return pl.pallas_call(
        attend_kernel,
        out_shape=(
            jax.ShapeDtypeStruct((2, RUN, HEAD), F32),
            jax.ShapeDtypeStruct((2, RUN, 2 * HEAD), BF16),
            jax.ShapeDtypeStruct((2, 1, RUN), F32),
        ),
        in_specs=[SMEM_SPEC, VMEM_SPEC],
        out_specs=(VMEM_SPEC,) * 3,
        scratch_shapes=[pltpu.VMEM((8, 8, RUN), F32)],
        compiler_params=pltpu.CompilerParams(vmem_limit_bytes=14 * 2**20),
        cost_estimate=pl.CostEstimate(
            flops=24 * 768 * 3072 * 64, bytes_accessed=3 * 2**20, transcendentals=768 * 3072
        ),
    )(x, recv)


def attend_back_kernel(
    x_ref, recv_ref, do_ref, mixed_ref, lse_ref, dq_ref, dkv_ref, codes_ref, acc_ref
):
    x = x_ref[0]
    acc_ref[...] = jnp.zeros_like(acc_ref)
    code_rows(recv_ref, codes_ref)
    for run in range(2):
        q = recv_ref[x, run][:, 2 * HEAD : 3 * HEAD] * SCALE
        do = do_ref[run][:, :HEAD]
        last = 4 * run + x
        qcodes = codes_ref[last]
        lse = lse_ref[run]
        inner = dot(
            jnp.ones((8, HEAD), F32), do.astype(F32) * mixed_ref[run], ((1,), (1,)), EXACT
        )[0:1]

        def block(kb, dq, diagonal):
            kv = recv_ref[lax.rem(kb, 4), kb // 4]
            keys = kv[:, :HEAD]
            kcode = code_cols(kv)
            scores = mm_nt(keys, q)
            if diagonal:
                rows = lax.broadcasted_iota(jnp.int32, (RUN, RUN), 0)
                cols = lax.broadcasted_iota(jnp.int32, (RUN, RUN), 1)
                allowed = (kcode == qcodes[0:1]) & (rows <= cols)
            else:
                allowed = kcode == qcodes[1:2]
            probs = jnp.where(allowed, jnp.exp(scores - lse), 0.0)
            grad_probs = mm_nt(kv[:, HEAD : 2 * HEAD], do)
            grad_raw = (probs * (grad_probs - inner)).astype(BF16)
            dk = mm(grad_raw, q)
            dv = mm(probs.astype(BF16), do)
            acc_ref[kb] += jnp.concatenate([dk, dv], axis=1)
            return dq + mm_tn(keys, grad_raw)

        dq = block(last, jnp.zeros((HEAD, RUN), F32), True)
        dq = lax.fori_loop(0, last, lambda kb, carry: block(kb, carry, False), dq)
        dq_ref[run] = (dq * SCALE).T.astype(BF16)
    for kb in range(8):
        dkv_ref[kb % 4, kb // 4] = acc_ref[kb].astype(BF16)


def attend_back(x, recv, do, mixed, lse):
    return pl.pallas_call(
        attend_back_kernel,
        out_shape=(
            jax.ShapeDtypeStruct((2, RUN, HEAD), BF16),
            jax.ShapeDtypeStruct((4, 2, RUN, 2 * HEAD), BF16),
        ),
        in_specs=[SMEM_SPEC] + [VMEM_SPEC] * 4,
        out_specs=(VMEM_SPEC,) * 2,
        scratch_shapes=[pltpu.VMEM((8, 8, RUN), F32), pltpu.VMEM((8, RUN, 2 * HEAD), F32)],
        compiler_params=pltpu.CompilerParams(vmem_limit_bytes=18 * 2**20),
        cost_estimate=pl.CostEstimate(
            flops=60 * 768 * 3072 * 64, bytes_accessed=6 * 2**20, transcendentals=768 * 3072
        ),
    )(x, recv, do, mixed, lse)


ROOT = 0.7978845608028654
CUBE = 0.044715


def feed_kernel(
    parts_ref, routed_ref, gate_ref, branch_ref, low_ref, grad_act_ref, gain_ref, bias_ref,
    core_ref, wo_hbm, we_hbm,
    kept_ref, given_ref, back_ref, projected_ref, hidden_ref, logit_ref, vector_ref, act_ref,
    wo_ref, we_ref, sems,
):
    copies = [pltpu.make_async_copy(wo_hbm, wo_ref, sems.at[4])]
    for i in range(4):
        cols = pl.ds(i * D, D)
        copies.append(pltpu.make_async_copy(we_hbm.at[:, cols], we_ref.at[i], sems.at[i]))
    for copy in copies:
        copy.start()
    mixed = jnp.concatenate([parts_ref[holder, :, :HEAD] for holder in HOLDERS], axis=1)
    copies[0].wait()
    projected = mm(mixed, wo_ref[...])
    projected_ref[...] = projected
    routed = routed_ref[...]
    gain = gain_ref[...]
    normed, unit, inv = layer_norm(routed + projected, gain, bias_ref[...])
    normed = normed.astype(BF16)
    grad_branch = branch_ref[...]
    grad_contracted = low_ref[...]
    grad_normed = jnp.zeros((SLOTS, D), F32)
    inner = jnp.sum(grad_branch * projected, axis=1, keepdims=True)
    for i in range(4):
        copies[i + 1].wait()
        v = mm(normed, we_ref[i])
        t = jnp.tanh(ROOT * (v + CUBE * v * v * v))
        half = 0.5 * (1.0 + t)
        act = v * half
        slope = half + 0.5 * v * (1.0 - t * t) * (ROOT * (1.0 + 3.0 * CUBE * v * v))
        grad_act = grad_act_ref[:, i * D : (i + 1) * D]
        inner += jnp.sum(act * grad_act, axis=1, keepdims=True)
        act = act.astype(BF16)
        grad_expanded = (grad_act * slope).astype(BF16)
        grad_normed += mm_nt(grad_expanded, we_ref[i])
        act_ref[:, i * D : (i + 1) * D] = act

        @pl.when(core_ref[0] == 0)
        def _(i=i, grad_expanded=grad_expanded, act=act):
            kept_ref[i, :, :D] = normed
            kept_ref[i, :, D : 2 * D] = grad_expanded
            given_ref[i, :, :D] = act
            given_ref[i, :, D : 2 * D] = grad_contracted

        @pl.when(core_ref[0] == 1)
        def _(i=i, grad_expanded=grad_expanded, act=act):
            given_ref[i, :, :D] = normed
            given_ref[i, :, D : 2 * D] = grad_expanded
            kept_ref[i, :, :D] = act
            kept_ref[i, :, D : 2 * D] = grad_contracted
    grad_logit = (1.0 - gate_ref[...]) * inner
    logit_ref[...] = grad_logit
    grad_hidden = layer_norm_back(grad_normed, unit, inv, gain)
    hidden_ref[...] = grad_hidden
    grad_projected = (grad_branch + grad_hidden).astype(BF16)
    grad_mixed = mm_nt(grad_projected, wo_ref[...]).astype(BF16)
    for head in range(HEADS):
        back_ref[HOLDERS[head], :, :HEAD] = grad_mixed[:, head * HEAD : (head + 1) * HEAD]
        back_ref[HOLDERS[head], :, HEAD:] = jnp.zeros((SLOTS, HEAD), BF16)
    for holder in IDLE:
        back_ref[holder] = jnp.zeros((SLOTS, 2 * HEAD), BF16)
    halves = (mixed[:, :384], mixed[:, 384:])
    for i in range(4):
        part = grad_projected[:, i * 192 : (i + 1) * 192]
        kept_ref[i, :, 2 * D + 384 :] = part
        given_ref[i, :, 2 * D + 384 :] = part
    for core in range(2):

        @pl.when(core_ref[0] == core)
        def _(core=core):
            for i in range(4):
                kept_ref[i, :, 2 * D : 2 * D + 384] = halves[core]
                given_ref[i, :, 2 * D : 2 * D + 384] = halves[1 - core]

    vector_ref[0:1] = jnp.sum(grad_logit * routed, axis=0, keepdims=True)
    vector_ref[1:2] = jnp.sum(grad_normed * unit, axis=0, keepdims=True)
    vector_ref[2:3] = jnp.sum(grad_normed, axis=0, keepdims=True)


def feed(parts, routed, gate, branch, low, grad_act, gain, bias, core, wo, we):
    return pl.pallas_call(
        feed_kernel,
        out_shape=(
            jax.ShapeDtypeStruct((4, SLOTS, 2 * D + 576), BF16),
            jax.ShapeDtypeStruct((4, SLOTS, 2 * D + 576), BF16),
            jax.ShapeDtypeStruct((16, SLOTS, 2 * HEAD), BF16),
            jax.ShapeDtypeStruct((SLOTS, D), F32),
            jax.ShapeDtypeStruct((SLOTS, D), F32),
            jax.ShapeDtypeStruct((SLOTS, 1), F32),
            jax.ShapeDtypeStruct((3, D), F32),
            jax.ShapeDtypeStruct((SLOTS, FF), BF16),
        ),
        in_specs=[VMEM_SPEC] * 8 + [SMEM_SPEC] + [HBM_SPEC] * 2,
        out_specs=(VMEM_SPEC,) * 8,
        scratch_shapes=[
            pltpu.VMEM((D, D), BF16),
            pltpu.VMEM((4, D, D), BF16),
            pltpu.SemaphoreType.DMA((5,)),
        ],
        compiler_params=pltpu.CompilerParams(vmem_limit_bytes=58 * 2**20),
        cost_estimate=pl.CostEstimate(
            flops=20 * SLOTS * D * D, bytes_accessed=10 * 2**20, transcendentals=SLOTS * FF
        ),
    )(parts, routed, gate, branch, low, grad_act, gain, bias, core, wo, we)


def unit_kernel(*refs):
    parts, (vector_ref, out_ref) = refs[:4], refs[4:]

    def outer(left, right):
        total = jnp.zeros((left.stop - left.start, right.stop - right.start), F32)
        for part in parts:
            total += mm_tn(part[:, left], part[:, right])
        return total.astype(BF16)

    tile = outer(slice(2 * D, 2 * D + 384), slice(2 * D + 384, 2 * D + 576))
    for block in range(2):
        unit = outer(slice(block * 384, (block + 1) * 384), slice(D, 2 * D))
        for i in range(8):
            at = block * 8 + i
            out_ref[at // 4, at % 4, :, :D] = unit[i * 48 : (i + 1) * 48]
            out_ref[at // 4, at % 4, :, D:] = jnp.concatenate(
                [
                    tile[(at // 2) * 48 : (at // 2 + 1) * 48, (at % 2) * 96 : (at % 2 + 1) * 96],
                    vector_ref[at],
                ],
                axis=1,
            )


def unit_grads(parts, vectors):
    return pl.pallas_call(
        unit_kernel,
        out_shape=jax.ShapeDtypeStruct((4, 4, 48, 896), BF16),
        in_specs=[VMEM_SPEC] * 5,
        out_specs=VMEM_SPEC,
        compiler_params=pltpu.CompilerParams(vmem_limit_bytes=14 * 2**20),
        cost_estimate=pl.CostEstimate(
            flops=2 * 384 * D * D, bytes_accessed=3 * 2**20, transcendentals=0
        ),
    )(*parts, vectors)


def embed_back_kernel(
    back_ref, routed_ref, hidden_ref, logit_ref, rows_ref, grad_ref, router_ref, gain_ref,
    wk_hbm, wv_hbm, wq_hbm, out_ref, w_ref, sems,
):
    copies = [
        pltpu.make_async_copy(w, w_ref.at[i], sems.at[i])
        for i, w in enumerate((wk_hbm, wv_hbm, wq_hbm))
    ]
    for copy in copies:
        copy.start()
    routed = routed_ref[...]
    gain = gain_ref[...].reshape(1, D)
    unused, unit, inv = layer_norm(routed, gain, 0.0)
    grad_normed = jnp.zeros((SLOTS, D), F32)
    for i in range(3):
        grads = jnp.concatenate(
            [back_ref[holder, :, i * HEAD : (i + 1) * HEAD] for holder in HOLDERS], axis=1
        )
        copies[i].wait()
        grad_normed += mm_nt(grads, w_ref[i])
    grad_rows = (
        logit_ref[...] * router_ref[...].reshape(1, D)
        + hidden_ref[...]
        + layer_norm_back(grad_normed, unit, inv, gain)
    )
    places = lax.broadcasted_iota(jnp.int32, (TOK, SLOTS), 0)
    picks = (rows_ref[...] == places).astype(F32)
    out_ref[...] = (
        grad_ref[...].astype(F32) + dot(picks, grad_rows, ((1,), (0,)), EXACT)
    ).astype(BF16)


def embed_back(back, routed, hidden, logit, rows, grad, router, gain, wk, wv, wq):
    return pl.pallas_call(
        embed_back_kernel,
        out_shape=jax.ShapeDtypeStruct((TOK, D), BF16),
        in_specs=[VMEM_SPEC] * 8 + [HBM_SPEC] * 3,
        out_specs=VMEM_SPEC,
        scratch_shapes=[pltpu.VMEM((3, D, D), BF16), pltpu.SemaphoreType.DMA((3,))],
        compiler_params=pltpu.CompilerParams(vmem_limit_bytes=58 * 2**20),
        cost_estimate=pl.CostEstimate(
            flops=6 * SLOTS * D * D, bytes_accessed=6 * 2**20, transcendentals=0
        ),
    )(back, routed, hidden, logit, rows, grad, router, gain, wk, wv, wq)


def body(
    tokens,
    router,
    gain_one,
    bias_one,
    w_query,
    w_key,
    w_value,
    w_out,
    gain_two,
    bias_two,
    w_expand,
    w_contract,
    cotangent,
    seq_ids,
    routed_rows,
    routed_count,
):
    x_at = lax.axis_index("x").astype(jnp.int32)
    core_at = lax.axis_index("c").astype(jnp.int32)
    y_at = lax.axis_index(("yh", "yl")).astype(jnp.int32)
    z_at = lax.axis_index("z").astype(jnp.int32)
    first_at = jnp.where(core_at == 0, x_at, z_at)
    second_at = jnp.where(core_at == 0, z_at, x_at)
    row_index = routed_rows[0, 0]
    routed_total = routed_count[0, 0]
    x_local = tokens[0]
    place_at = lax.axis_index(("z", "c")).astype(jnp.int32)
    to_heads, normed_low, routed_x = embed(
        jnp.stack([routed_total, place_at]),
        routed_rows[0],
        seq_ids,
        x_local,
        gain_one,
        bias_one,
        w_key,
        w_value,
        w_query,
    )
    recv = swap(to_heads.reshape(64, SLOTS, 4 * HEAD), ("x",) + SIXTEEN)
    w_part = jnp.concatenate(
        [
            lax.dynamic_slice(
                w,
                (lax.axis_index(("x", "z", "yl")) * 24, (core_at * 2 + lax.axis_index("yh")) * 3 * HEAD),
                (24, 3 * HEAD),
            )
            for w in (w_key, w_value, w_query)
        ],
        axis=1,
    ).astype(F32)
    recv, w_part = lax.optimization_barrier((recv, w_part))
    recv = recv.reshape(4, 2, RUN, 4 * HEAD)
    normed_block = lax.all_gather(normed_low, SIXTEEN, axis=0, tiled=True)

    is_valid = jnp.arange(SLOTS, dtype=jnp.int32) < routed_total
    picks = row_index[:, None] == jnp.arange(TOK, dtype=jnp.int32)[None, :]
    pick_low = picks.astype(BF16)
    pick_full = picks.astype(F32)
    gate_value = jax.nn.sigmoid(jnp.sum(routed_x * router[None, :], axis=-1))
    gate_used = jnp.where(is_valid, gate_value, 0.0)
    grad_local = cotangent[0]
    grad_branch = gate_used[:, None] * mm(pick_low, grad_local)
    grad_contracted = grad_branch.astype(BF16)
    grad_activated = mm_nt(grad_contracted, w_contract)

    mixed_here, mixed_low, lse = attend(x_at[None], recv)
    mixed_parts = swap(mixed_low.reshape(16, SLOTS, 2 * HEAD), SIXTEEN)
    (kept, given, do_parts, projected, grad_hidden, grad_logit, vectors, activated_low) = feed(
        mixed_parts,
        routed_x,
        gate_value[:, None],
        grad_branch,
        grad_contracted,
        grad_activated,
        gain_two[None],
        bias_two[None],
        core_at[None],
        w_out,
        w_expand,
    )
    given = lax.ppermute(given, "c", [(0, 1), (1, 0)])
    eight = jnp.concatenate([kept, given], axis=1)
    eight = ring_swap(eight, first_at, lambda step: ring_pairs(0, step), CUBE_AXES)
    do_parts = swap(do_parts, SIXTEEN)
    eight, do_parts, normed_block = lax.optimization_barrier((eight, do_parts, normed_block))
    vectors = jnp.pad(vectors.astype(BF16).reshape(16, 48, 3), ((0, 0), (0, 0), (0, 29)))
    partial_grads = unit_grads(eight, vectors)
    do_parts, partial_grads = lax.optimization_barrier((do_parts, partial_grads))
    grad_q, grad_kv = attend_back(
        x_at[None], recv, do_parts.reshape(2, RUN, 2 * HEAD), mixed_here, lse
    )
    partial_grads = ring_swap(
        partial_grads, second_at, lambda step: ring_pairs(1, step), CUBE_AXES
    )
    partial_grads, grad_kv = lax.optimization_barrier((partial_grads, grad_kv))
    partial_grads = sum(part.astype(F32) for part in partial_grads).astype(BF16)
    partial_grads = ring_swap(
        partial_grads,
        y_at,
        lambda step: [(i, (i + step) % 4) for i in range(4)],
        ("yh", "yl"),
    )
    own_grads = sum(part.astype(F32) for part in partial_grads).astype(BF16)
    grad_kv, own_grads = lax.optimization_barrier((grad_kv, own_grads))
    grad_kv = swap(grad_kv, ("x",))
    grad_kv_sum = jnp.sum(grad_kv.astype(F32), axis=0).astype(BF16)
    grad_heads = jnp.concatenate(
        [grad_kv_sum.reshape(2 * RUN, 2 * HEAD), grad_q.reshape(2 * RUN, HEAD)], axis=1
    )
    units = lax.all_gather(own_grads, CHIPS, axis=0, tiled=False)
    branch = projected + mm(activated_low, w_contract)
    output = (
        x_local.astype(F32)
        + dot(pick_full, gate_used[:, None] * branch, ((0,), (0,)), EXACT)
    ).astype(BF16)

    grad_qkv = mm_tn(normed_block, grad_heads).astype(BF16).reshape(32, 24, 3 * HEAD)
    column_sum = jnp.sum(grad_heads.astype(F32), axis=0).astype(BF16)
    column_sum = jnp.broadcast_to(column_sum[None, None, :], (32, 8, 3 * HEAD))
    grad_qkv = swap(jnp.concatenate([grad_qkv, column_sum], axis=1), ("x", "z", "yl"))
    grad_qkv, output = lax.optimization_barrier((grad_qkv, output))
    grad_qkv = jnp.sum(grad_qkv.reshape(4, 4, 2, 32, 3 * HEAD)[:, :3].astype(F32), axis=(0, 2))
    grad_qkv = jnp.concatenate(
        [
            grad_qkv[:, :, kind * HEAD : (kind + 1) * HEAD].transpose(1, 0, 2).reshape(32, 3 * HEAD)
            for kind in range(3)
        ],
        axis=1,
    )
    column_sum = grad_qkv[24]
    grad_qkv = grad_qkv[:24]
    norm_sums = jnp.stack(
        [jnp.sum(w_part * grad_qkv, axis=1), jnp.sum(w_part * column_sum[None, :], axis=1)], axis=1
    )
    own_qkv = jnp.concatenate([grad_qkv, jnp.pad(norm_sums, ((0, 0), (0, 62)))], axis=1)
    own_qkv = own_qkv.astype(BF16)
    heads = spread(own_qkv, CHIPS)
    heads, grad_heads = lax.optimization_barrier((heads, grad_heads))
    back = swap(
        jnp.pad(grad_heads, ((0, 0), (0, HEAD))).reshape(16, SLOTS, 4 * HEAD), SIXTEEN
    )
    heads_other = lax.ppermute(heads, "c", [(0, 1), (1, 0)])
    me = jnp.stack([x_at, y_at, z_at, core_at])
    final_key, final_value, final_query, norm_sums = place_heads(me, heads, heads_other)
    norm_sums = norm_sums[:, :2].T
    grad_gain_one = (norm_sums[0] - bias_one * norm_sums[1]) / gain_one
    grad_bias_one = norm_sums[1]
    units, back, final_key, grad_gain_one = lax.optimization_barrier(
        (units, back, final_key, grad_gain_one)
    )
    first = place(me, units)
    back, first = lax.optimization_barrier((back, first))
    input_grad = embed_back(
        back,
        routed_x,
        grad_hidden,
        grad_logit,
        routed_rows[0],
        grad_local,
        router,
        gain_one,
        w_key,
        w_value,
        w_query,
    )
    placed = place(me, other_core([units])[0], first)
    final_expand, final_contract, final_out = placed[:3]
    vectors = first[3] + placed[3]
    vectors = vectors[:, :, :3].reshape(3, D)
    return (
        output[None],
        input_grad[None],
        vectors[0],
        grad_gain_one,
        grad_bias_one,
        final_query,
        final_key,
        final_value,
        final_out,
        vectors[1],
        vectors[2],
        final_expand,
        final_contract,
    )


def solution(mesh):
    fine = Mesh(mesh.devices.reshape(2, 4, 4, 2, 2), ("yh", "x", "z", "c", "yl"))
    seq = ("yh", "x", "z", "c")
    in_specs = (
        (P("yl", seq, None),)
        + (P(),) * 11
        + (P("yl", seq, None), P("yl", seq), P("yl", seq, None), P("yl", seq))
    )
    out_specs = (P("yl", seq, None),) * 2 + (P(),) * 11
    return jax.shard_map(body, mesh=fine, in_specs=in_specs, out_specs=out_specs, check_vma=False)
```

```python
import functools

import jax
import jax.numpy as jnp
from jax import lax
from jax.experimental import pallas as pl
from jax.experimental.pallas import tpu as pltpu
from jax.sharding import Mesh
from jax.sharding import PartitionSpec as P

HEAD = 64
HEADS = 12
SLOTS = 48
D = 768
FF = 3072
TOK = 256
RUN = 384
EPSILON = 1e-05
NEG_LARGE = -1e30
EXACT = lax.Precision.HIGHEST
SCALE = float(HEAD) ** (-0.5)
F32 = jnp.float32
BF16 = jnp.bfloat16

SIXTEEN = ("yh", "z", "c")
HOLDERS = [yh * 8 + z * 2 + c for c in range(2) for yh in range(2) for z in range(3)]
IDLE = [yh * 8 + 6 + c for yh in range(2) for c in range(2)]
SIZES = {"yh": 2, "x": 4, "z": 4, "c": 2, "yl": 2}


def width_of(axes):
    total = 1
    for axis in axes:
        total *= SIZES[axis]
    return total


def swap(parts, axes):
    return lax.all_to_all(parts, axes, split_axis=0, concat_axis=0, tiled=True)


def spread(part, axes):
    parts = width_of(axes)
    return swap(jnp.broadcast_to(part[None], (parts,) + part.shape), axes)


CHIPS = ("x", "yh", "yl", "z")
SMEM_SPEC = pl.BlockSpec(memory_space=pltpu.SMEM)
ANY_SPEC = pl.BlockSpec(memory_space=pl.ANY)
VMEM_SPEC = pl.BlockSpec(memory_space=pltpu.VMEM)
HBM_SPEC = pl.BlockSpec(memory_space=pltpu.HBM)


CUBE_AXES = ("x", "z", "c")
FIRST = (("x", "z"), ("z", "x"))


def ring_pairs(turn, step):
    pairs = []
    for x in range(4):
        for z in range(4):
            for c in range(2):
                to = {"x": x, "z": z}
                axis = FIRST[c][turn]
                to[axis] = (to[axis] + step) % 4
                pairs.append((x * 8 + z * 2 + c, to["x"] * 8 + to["z"] * 2 + c))
    return pairs


def ring_swap(parts, at, pairs_of, axes):
    mine = [lax.dynamic_index_in_dim(parts, at, 0, keepdims=False)]
    for step in (1, 2, 3):
        part = lax.dynamic_index_in_dim(parts, lax.rem(at + step, 4), 0, keepdims=False)
        mine.append(lax.ppermute(part, axes, pairs_of(step)))
    return mine


def other_core(pieces):
    return [lax.ppermute(piece, "c", [(0, 1), (1, 0)]) for piece in pieces]


def dot(left, right, dims, precision=None):
    return lax.dot_general(
        left, right, (dims, ((), ())), precision=precision, preferred_element_type=F32
    )


def mm(left, right):
    return dot(left, right, ((1,), (0,)))


def mm_tn(left, right):
    return dot(left, right, ((0,), (0,)))


def mm_nt(left, right):
    return dot(left, right, ((1,), (1,)))


def layer_norm(values_in, gain_vec, bias_vec):
    center = values_in - jnp.mean(values_in, axis=-1, keepdims=True)
    spread_ = jnp.mean(center * center, axis=-1, keepdims=True)
    inv = lax.rsqrt(spread_ + EPSILON)
    unit = center * inv
    return unit * gain_vec + bias_vec, unit, inv


def layer_norm_back(grad, unit, inv, gain_vec):
    scaled = grad * gain_vec
    mean_one = jnp.mean(scaled, axis=-1, keepdims=True)
    mean_two = jnp.mean(scaled * unit, axis=-1, keepdims=True)
    return inv * (scaled - mean_one - unit * mean_two)


def place_kernel(
    other, me_ref, units_in, *refs
):
    if other:
        refs = refs[3:]
    (
        expand_ref, contract_ref, out_ref, vector_ref,
        land_ref, stage_ref, tiles_ref, in_sems, out_sems,
    ) = refs

    def take(x):
        rows = pl.ds(x * 16, 16)
        return pltpu.make_async_copy(units_in.at[rows], land_ref.at[rows], in_sems.at[x])

    for x in range(4):
        take(x).start()

    def emit(core):
        for x in range(4):
            take(x).wait()
            for y in range(4):
                for z in range(4):
                    staged = stage_ref.at[x, y * 4 + z]
                    staged[...] = land_ref[x * 16 + y * 4 + z, :, :D].astype(F32)
                    if core == 0:
                        target = expand_ref.at[pl.ds((z * 4 + y) * 48, 48), pl.ds(x * D, D)]
                    else:
                        target = contract_ref.at[pl.ds(z * D + (x * 4 + y) * 48, 48), :]
                    pltpu.make_async_copy(staged, target, out_sems.at[x]).start()

        def unit_shard(unit, at16):
            if core == 0:
                x, y, z = unit, at16 % 4, at16 // 4
            else:
                x, y, z = at16 // 4, at16 % 4, unit
            return land_ref[x * 16 + y * 4 + z, :, D:].astype(F32)

        for row in range(8):
            tiles_ref[row * 48 : (row + 1) * 48, :] = jnp.concatenate(
                [
                    unit_shard(unit, row * 2 + half)[:, :96]
                    for unit in range(4)
                    for half in range(2)
                ],
                axis=1,
            )
        copy = pltpu.make_async_copy(
            tiles_ref, out_ref.at[pl.ds(core * 384, 384), :], out_sems.at[4]
        )
        copy.start()
        for at16 in range(16):
            vector_ref[at16] = sum(unit_shard(unit, at16)[:, 96:] for unit in range(4))
        for x in range(4):
            held = stage_ref.at[x]
            pltpu.make_async_copy(held, held, out_sems.at[x]).wait()
        copy.wait()

    for core in range(2):
        pl.when((me_ref[3] + other & 1) == core)(functools.partial(emit, core))


def place(me, units, before=None):
    before = () if before is None else tuple(before[:3])
    return pl.pallas_call(
        functools.partial(place_kernel, 1 if before else 0),
        out_shape=(
            jax.ShapeDtypeStruct((D, FF), F32),
            jax.ShapeDtypeStruct((FF, D), F32),
            jax.ShapeDtypeStruct((D, D), F32),
            jax.ShapeDtypeStruct((16, 48, 32), F32),
        ),
        in_specs=[SMEM_SPEC, ANY_SPEC] + [ANY_SPEC] * len(before),
        out_specs=(ANY_SPEC,) * 3 + (VMEM_SPEC,),
        scratch_shapes=[
            pltpu.VMEM((64, 48, 896), BF16),
            pltpu.VMEM((4, 16, 48, D), F32),
            pltpu.VMEM((384, D), F32),
            pltpu.SemaphoreType.DMA((4,)),
            pltpu.SemaphoreType.DMA((5,)),
        ],
        input_output_aliases={2 + i: i for i in range(3)} if before else {},
        compiler_params=pltpu.CompilerParams(vmem_limit_bytes=32 * 2**20),
        cost_estimate=pl.CostEstimate(flops=0, bytes_accessed=20 * 2**20, transcendentals=0),
    )(me, units, *before)


def place_heads_kernel(me_ref, own_ref, other_ref, key_ref, value_ref, query_ref, sums_ref):
    def emit(by_core):
        for x in range(4):
            for z in range(4):
                for yl in range(2):
                    blocks = [
                        by_core[c][x * 16 + (yh * 2 + yl) * 4 + z].astype(F32)
                        for c in range(2)
                        for yh in range(2)
                    ]
                    at = ((x * 4 + z) * 2 + yl) * 24
                    for kind, out_ref in enumerate((key_ref, value_ref, query_ref)):
                        out_ref[at : at + 24, :] = jnp.concatenate(
                            [block[:, kind * 192 : (kind + 1) * 192] for block in blocks], axis=1
                        )
                    sums_ref[at : at + 24, :] = sum(block[:, 576:] for block in blocks)

    @pl.when(me_ref[3] == 0)
    def _():
        emit((own_ref, other_ref))

    @pl.when(me_ref[3] == 1)
    def _():
        emit((other_ref, own_ref))


def place_heads(me, own, other):
    return pl.pallas_call(
        place_heads_kernel,
        out_shape=(jax.ShapeDtypeStruct((D, D), F32),) * 3
        + (jax.ShapeDtypeStruct((D, HEAD), F32),),
        in_specs=[SMEM_SPEC] + [VMEM_SPEC] * 2,
        out_specs=(VMEM_SPEC,) * 4,
        compiler_params=pltpu.CompilerParams(vmem_limit_bytes=18 * 2**20),
        cost_estimate=pl.CostEstimate(flops=0, bytes_accessed=12 * 2**20, transcendentals=0),
    )(me, own, other)


def embed_kernel(
    count_ref, rows_ref, ids_ref, tokens_ref, gain_ref, bias_ref, wk_hbm, wv_hbm, wq_hbm,
    chunk_ref, normed_ref, routed_ref, w_ref, sems,
):
    for i, w in enumerate((wk_hbm, wv_hbm, wq_hbm)):
        pltpu.make_async_copy(w, w_ref.at[i], sems.at[i]).start()
    places = lax.broadcasted_iota(jnp.int32, (TOK, SLOTS), 0)
    picks = (rows_ref[...] == places).astype(F32).astype(BF16)
    routed = mm_tn(picks, tokens_ref[...])
    gain = gain_ref[...].reshape(1, D)
    bias = bias_ref[...].reshape(1, D)
    normed = layer_norm(routed, gain, bias)[0].astype(BF16)
    routed_ref[...] = routed
    normed_ref[...] = normed
    ids = ids_ref[...]
    halves = jnp.concatenate([ids >> 8, ids & 255] + [jnp.zeros((6, TOK), jnp.int32)], axis=0)
    halves = halves.astype(F32).astype(BF16)
    ids_rows = mm(halves, picks)
    ids_cols = dot(picks, halves, ((0,), (1,)))
    ids_row = ids_rows[0:1] * 256.0 + ids_rows[1:2]
    ids_col = ids_cols[:, 0:1] * 256.0 + ids_cols[:, 1:2]
    slot_row = lax.broadcasted_iota(jnp.int32, (SLOTS, SLOTS), 1)
    slot_col = lax.broadcasted_iota(jnp.int32, (SLOTS, SLOTS), 0)
    count = count_ref[0]
    same = (ids_row == ids_col) & (slot_row < count) & (slot_col < count) | (slot_row == slot_col)
    first = jnp.min(
        jnp.where(same, slot_row.astype(F32), float(SLOTS)), axis=1, keepdims=True
    )
    lanes = lax.broadcasted_iota(jnp.int32, (SLOTS, HEAD), 1)
    slots = lax.broadcasted_iota(jnp.int32, (SLOTS, HEAD), 0)
    is_long = (ids_col == 0.0) & (slots < count)
    marks = jnp.where(lanes == 0, first + 1.0, jnp.where(lanes == 1, count_ref[1] + 1.0, 0.0))
    marks = jnp.where(is_long, 0.0, marks).astype(BF16)
    parts = []
    for i in range(3):
        pltpu.make_async_copy((wk_hbm, wv_hbm, wq_hbm)[i], w_ref.at[i], sems.at[i]).wait()
        parts.append(mm(normed, w_ref[i]).astype(BF16))
    for head in range(HEADS):
        cols = slice(head * HEAD, (head + 1) * HEAD)
        chunk = jnp.concatenate([part[:, cols] for part in parts] + [marks], axis=1)
        for x in range(4):
            chunk_ref[x, HOLDERS[head]] = chunk
    for x in range(4):
        for holder in IDLE:
            chunk_ref[x, holder] = jnp.zeros((SLOTS, 4 * HEAD), BF16)


def embed(scalars, rows, ids, tokens, gain, bias, wk, wv, wq):
    return pl.pallas_call(
        embed_kernel,
        out_shape=(
            jax.ShapeDtypeStruct((4, 16, SLOTS, 4 * HEAD), BF16),
            jax.ShapeDtypeStruct((SLOTS, D), BF16),
            jax.ShapeDtypeStruct((SLOTS, D), F32),
        ),
        in_specs=[SMEM_SPEC] + [VMEM_SPEC] * 5 + [HBM_SPEC] * 3,
        out_specs=(VMEM_SPEC,) * 3,
        scratch_shapes=[pltpu.VMEM((3, D, D), BF16), pltpu.SemaphoreType.DMA((3,))],
        compiler_params=pltpu.CompilerParams(vmem_limit_bytes=58 * 2**20),
        cost_estimate=pl.CostEstimate(
            flops=6 * SLOTS * D * D, bytes_accessed=6 * 2**20, transcendentals=0
        ),
    )(scalars, rows, ids, tokens, gain, bias, wk, wv, wq)


def code_rows(recv_ref, codes_ref):
    lane = lax.broadcasted_iota(jnp.int32, (8, HEAD), 1)
    pick = jnp.where(lane == 0, 1.0, jnp.where(lane == 1, 64.0, 0.0)).astype(BF16)
    for kb in range(8):
        codes = mm_nt(pick, recv_ref[kb % 4, kb // 4, :, 3 * HEAD :])
        row = lax.broadcasted_iota(jnp.int32, (8, RUN), 0)
        codes_ref[kb] = jnp.where((row == 1) & (codes > 0.0), -1.0, codes)


def code_cols(block):
    marks = block[:, 3 * HEAD :].astype(F32)
    return marks[:, 0:1] + 64.0 * marks[:, 1:2]


def attend_kernel(x_ref, recv_ref, out_ref, low_ref, lse_ref, codes_ref):
    x = x_ref[0]
    code_rows(recv_ref, codes_ref)
    for run in range(2):
        q = recv_ref[x, run][:, 2 * HEAD : 3 * HEAD] * SCALE
        last = 4 * run + x
        qcodes = codes_ref[last]

        def block(kb, carry, diagonal):
            peak, total, acc = carry
            kv = recv_ref[lax.rem(kb, 4), kb // 4]
            kcode = code_cols(kv)
            scores = mm_nt(kv[:, :HEAD], q)
            if diagonal:
                rows = lax.broadcasted_iota(jnp.int32, (RUN, RUN), 0)
                cols = lax.broadcasted_iota(jnp.int32, (RUN, RUN), 1)
                allowed = (kcode == qcodes[0:1]) & (rows <= cols)
            else:
                allowed = kcode == qcodes[1:2]
            scores = jnp.where(allowed, scores, NEG_LARGE)
            new_peak = jnp.maximum(peak, jnp.max(scores, axis=0, keepdims=True))
            probs = jnp.exp(scores - new_peak)
            decay = jnp.exp(peak - new_peak)
            total = total * decay + jnp.sum(probs, axis=0, keepdims=True)
            acc = acc * decay + mm_tn(kv[:, HEAD : 2 * HEAD], probs.astype(BF16))
            return new_peak, total, acc

        start = (
            jnp.full((1, RUN), NEG_LARGE, F32),
            jnp.zeros((1, RUN), F32),
            jnp.zeros((HEAD, RUN), F32),
        )
        carry = block(last, start, True)
        peak, total, acc = lax.fori_loop(
            0, last, lambda kb, carry: block(kb, carry, False), carry
        )
        mixed = (acc / total).T
        out_ref[run] = mixed
        low_ref[run, :, :HEAD] = mixed.astype(BF16)
        low_ref[run, :, HEAD:] = jnp.zeros((RUN, HEAD), BF16)
        lse_ref[run] = peak + jnp.log(total)


def attend(x, recv):
    return pl.pallas_call(
        attend_kernel,
        out_shape=(
            jax.ShapeDtypeStruct((2, RUN, HEAD), F32),
            jax.ShapeDtypeStruct((2, RUN, 2 * HEAD), BF16),
            jax.ShapeDtypeStruct((2, 1, RUN), F32),
        ),
        in_specs=[SMEM_SPEC, VMEM_SPEC],
        out_specs=(VMEM_SPEC,) * 3,
        scratch_shapes=[pltpu.VMEM((8, 8, RUN), F32)],
        compiler_params=pltpu.CompilerParams(vmem_limit_bytes=14 * 2**20),
        cost_estimate=pl.CostEstimate(
            flops=24 * 768 * 3072 * 64, bytes_accessed=3 * 2**20, transcendentals=768 * 3072
        ),
    )(x, recv)


def attend_back_kernel(
    x_ref, recv_ref, do_ref, mixed_ref, lse_ref, dq_ref, dkv_ref, codes_ref, acc_ref
):
    x = x_ref[0]
    acc_ref[...] = jnp.zeros_like(acc_ref)
    code_rows(recv_ref, codes_ref)
    for run in range(2):
        q = recv_ref[x, run][:, 2 * HEAD : 3 * HEAD] * SCALE
        do = do_ref[run][:, :HEAD]
        last = 4 * run + x
        qcodes = codes_ref[last]
        lse = lse_ref[run]
        inner = dot(
            jnp.ones((8, HEAD), F32), do.astype(F32) * mixed_ref[run], ((1,), (1,)), EXACT
        )[0:1]

        def block(kb, dq, diagonal):
            kv = recv_ref[lax.rem(kb, 4), kb // 4]
            keys = kv[:, :HEAD]
            kcode = code_cols(kv)
            scores = mm_nt(keys, q)
            if diagonal:
                rows = lax.broadcasted_iota(jnp.int32, (RUN, RUN), 0)
                cols = lax.broadcasted_iota(jnp.int32, (RUN, RUN), 1)
                allowed = (kcode == qcodes[0:1]) & (rows <= cols)
            else:
                allowed = kcode == qcodes[1:2]
            probs = jnp.where(allowed, jnp.exp(scores - lse), 0.0)
            grad_probs = mm_nt(kv[:, HEAD : 2 * HEAD], do)
            grad_raw = (probs * (grad_probs - inner)).astype(BF16)
            dk = mm(grad_raw, q)
            dv = mm(probs.astype(BF16), do)
            acc_ref[kb] += jnp.concatenate([dk, dv], axis=1)
            return dq + mm_tn(keys, grad_raw)

        dq = block(last, jnp.zeros((HEAD, RUN), F32), True)
        dq = lax.fori_loop(0, last, lambda kb, carry: block(kb, carry, False), dq)
        dq_ref[run] = (dq * SCALE).T.astype(BF16)
    for kb in range(8):
        dkv_ref[kb % 4, kb // 4] = acc_ref[kb].astype(BF16)


def attend_back(x, recv, do, mixed, lse):
    return pl.pallas_call(
        attend_back_kernel,
        out_shape=(
            jax.ShapeDtypeStruct((2, RUN, HEAD), BF16),
            jax.ShapeDtypeStruct((4, 2, RUN, 2 * HEAD), BF16),
        ),
        in_specs=[SMEM_SPEC] + [VMEM_SPEC] * 4,
        out_specs=(VMEM_SPEC,) * 2,
        scratch_shapes=[pltpu.VMEM((8, 8, RUN), F32), pltpu.VMEM((8, RUN, 2 * HEAD), F32)],
        compiler_params=pltpu.CompilerParams(vmem_limit_bytes=18 * 2**20),
        cost_estimate=pl.CostEstimate(
            flops=60 * 768 * 3072 * 64, bytes_accessed=6 * 2**20, transcendentals=768 * 3072
        ),
    )(x, recv, do, mixed, lse)


ROOT = 0.7978845608028654
CUBE = 0.044715


def feed_kernel(
    parts_ref, routed_ref, gate_ref, branch_ref, low_ref, grad_act_ref, gain_ref, bias_ref,
    core_ref, wo_hbm, we_hbm,
    kept_ref, given_ref, back_ref, projected_ref, hidden_ref, logit_ref, vector_ref, act_ref,
    wo_ref, we_ref, sems,
):
    copies = [pltpu.make_async_copy(wo_hbm, wo_ref, sems.at[4])]
    for i in range(4):
        cols = pl.ds(i * D, D)
        copies.append(pltpu.make_async_copy(we_hbm.at[:, cols], we_ref.at[i], sems.at[i]))
    for copy in copies:
        copy.start()
    mixed = jnp.concatenate([parts_ref[holder, :, :HEAD] for holder in HOLDERS], axis=1)
    copies[0].wait()
    projected = mm(mixed, wo_ref[...])
    projected_ref[...] = projected
    routed = routed_ref[...]
    gain = gain_ref[...]
    normed, unit, inv = layer_norm(routed + projected, gain, bias_ref[...])
    normed = normed.astype(BF16)
    grad_branch = branch_ref[...]
    grad_contracted = low_ref[...]
    grad_normed = jnp.zeros((SLOTS, D), F32)
    inner = jnp.sum(grad_branch * projected, axis=1, keepdims=True)
    for i in range(4):
        copies[i + 1].wait()
        v = mm(normed, we_ref[i])
        t = jnp.tanh(ROOT * (v + CUBE * v * v * v))
        half = 0.5 * (1.0 + t)
        act = v * half
        slope = half + 0.5 * v * (1.0 - t * t) * (ROOT * (1.0 + 3.0 * CUBE * v * v))
        grad_act = grad_act_ref[:, i * D : (i + 1) * D]
        inner += jnp.sum(act * grad_act, axis=1, keepdims=True)
        act = act.astype(BF16)
        grad_expanded = (grad_act * slope).astype(BF16)
        grad_normed += mm_nt(grad_expanded, we_ref[i])
        act_ref[:, i * D : (i + 1) * D] = act

        @pl.when(core_ref[0] == 0)
        def _(i=i, grad_expanded=grad_expanded, act=act):
            kept_ref[i, :, :D] = normed
            kept_ref[i, :, D : 2 * D] = grad_expanded
            given_ref[i, :, :D] = act
            given_ref[i, :, D : 2 * D] = grad_contracted

        @pl.when(core_ref[0] == 1)
        def _(i=i, grad_expanded=grad_expanded, act=act):
            given_ref[i, :, :D] = normed
            given_ref[i, :, D : 2 * D] = grad_expanded
            kept_ref[i, :, :D] = act
            kept_ref[i, :, D : 2 * D] = grad_contracted
    grad_logit = (1.0 - gate_ref[...]) * inner
    logit_ref[...] = grad_logit
    grad_hidden = layer_norm_back(grad_normed, unit, inv, gain)
    hidden_ref[...] = grad_hidden
    grad_projected = (grad_branch + grad_hidden).astype(BF16)
    grad_mixed = mm_nt(grad_projected, wo_ref[...]).astype(BF16)
    for head in range(HEADS):
        back_ref[HOLDERS[head], :, :HEAD] = grad_mixed[:, head * HEAD : (head + 1) * HEAD]
        back_ref[HOLDERS[head], :, HEAD:] = jnp.zeros((SLOTS, HEAD), BF16)
    for holder in IDLE:
        back_ref[holder] = jnp.zeros((SLOTS, 2 * HEAD), BF16)
    halves = (mixed[:, :384], mixed[:, 384:])
    for i in range(4):
        part = grad_projected[:, i * 192 : (i + 1) * 192]
        kept_ref[i, :, 2 * D + 384 :] = part
        given_ref[i, :, 2 * D + 384 :] = part
    for core in range(2):

        @pl.when(core_ref[0] == core)
        def _(core=core):
            for i in range(4):
                kept_ref[i, :, 2 * D : 2 * D + 384] = halves[core]
                given_ref[i, :, 2 * D : 2 * D + 384] = halves[1 - core]

    vector_ref[0:1] = jnp.sum(grad_logit * routed, axis=0, keepdims=True)
    vector_ref[1:2] = jnp.sum(grad_normed * unit, axis=0, keepdims=True)
    vector_ref[2:3] = jnp.sum(grad_normed, axis=0, keepdims=True)


def feed(parts, routed, gate, branch, low, grad_act, gain, bias, core, wo, we):
    return pl.pallas_call(
        feed_kernel,
        out_shape=(
            jax.ShapeDtypeStruct((4, SLOTS, 2 * D + 576), BF16),
            jax.ShapeDtypeStruct((4, SLOTS, 2 * D + 576), BF16),
            jax.ShapeDtypeStruct((16, SLOTS, 2 * HEAD), BF16),
            jax.ShapeDtypeStruct((SLOTS, D), F32),
            jax.ShapeDtypeStruct((SLOTS, D), F32),
            jax.ShapeDtypeStruct((SLOTS, 1), F32),
            jax.ShapeDtypeStruct((3, D), F32),
            jax.ShapeDtypeStruct((SLOTS, FF), BF16),
        ),
        in_specs=[VMEM_SPEC] * 8 + [SMEM_SPEC] + [HBM_SPEC] * 2,
        out_specs=(VMEM_SPEC,) * 8,
        scratch_shapes=[
            pltpu.VMEM((D, D), BF16),
            pltpu.VMEM((4, D, D), BF16),
            pltpu.SemaphoreType.DMA((5,)),
        ],
        compiler_params=pltpu.CompilerParams(vmem_limit_bytes=58 * 2**20),
        cost_estimate=pl.CostEstimate(
            flops=20 * SLOTS * D * D, bytes_accessed=10 * 2**20, transcendentals=SLOTS * FF
        ),
    )(parts, routed, gate, branch, low, grad_act, gain, bias, core, wo, we)


def unit_kernel(*refs):
    parts, (vector_ref, out_ref) = refs[:4], refs[4:]

    def outer(left, right):
        total = jnp.zeros((left.stop - left.start, right.stop - right.start), F32)
        for part in parts:
            total += mm_tn(part[:, left], part[:, right])
        return total.astype(BF16)

    tile = outer(slice(2 * D, 2 * D + 384), slice(2 * D + 384, 2 * D + 576))
    for block in range(2):
        unit = outer(slice(block * 384, (block + 1) * 384), slice(D, 2 * D))
        for i in range(8):
            at = block * 8 + i
            out_ref[at // 4, at % 4, :, :D] = unit[i * 48 : (i + 1) * 48]
            out_ref[at // 4, at % 4, :, D:] = jnp.concatenate(
                [
                    tile[(at // 2) * 48 : (at // 2 + 1) * 48, (at % 2) * 96 : (at % 2 + 1) * 96],
                    vector_ref[at],
                ],
                axis=1,
            )


def unit_grads(parts, vectors):
    return pl.pallas_call(
        unit_kernel,
        out_shape=jax.ShapeDtypeStruct((4, 4, 48, 896), BF16),
        in_specs=[VMEM_SPEC] * 5,
        out_specs=VMEM_SPEC,
        compiler_params=pltpu.CompilerParams(vmem_limit_bytes=14 * 2**20),
        cost_estimate=pl.CostEstimate(
            flops=2 * 384 * D * D, bytes_accessed=3 * 2**20, transcendentals=0
        ),
    )(*parts, vectors)


def embed_back_kernel(
    back_ref, routed_ref, hidden_ref, logit_ref, rows_ref, grad_ref, router_ref, gain_ref,
    wk_hbm, wv_hbm, wq_hbm, out_ref, w_ref, sems,
):
    copies = [
        pltpu.make_async_copy(w, w_ref.at[i], sems.at[i])
        for i, w in enumerate((wk_hbm, wv_hbm, wq_hbm))
    ]
    for copy in copies:
        copy.start()
    routed = routed_ref[...]
    gain = gain_ref[...].reshape(1, D)
    unused, unit, inv = layer_norm(routed, gain, 0.0)
    grad_normed = jnp.zeros((SLOTS, D), F32)
    for i in range(3):
        grads = jnp.concatenate(
            [back_ref[holder, :, i * HEAD : (i + 1) * HEAD] for holder in HOLDERS], axis=1
        )
        copies[i].wait()
        grad_normed += mm_nt(grads, w_ref[i])
    grad_rows = (
        logit_ref[...] * router_ref[...].reshape(1, D)
        + hidden_ref[...]
        + layer_norm_back(grad_normed, unit, inv, gain)
    )
    places = lax.broadcasted_iota(jnp.int32, (TOK, SLOTS), 0)
    picks = (rows_ref[...] == places).astype(F32)
    out_ref[...] = (
        grad_ref[...].astype(F32) + dot(picks, grad_rows, ((1,), (0,)), EXACT)
    ).astype(BF16)


def embed_back(back, routed, hidden, logit, rows, grad, router, gain, wk, wv, wq):
    return pl.pallas_call(
        embed_back_kernel,
        out_shape=jax.ShapeDtypeStruct((TOK, D), BF16),
        in_specs=[VMEM_SPEC] * 8 + [HBM_SPEC] * 3,
        out_specs=VMEM_SPEC,
        scratch_shapes=[pltpu.VMEM((3, D, D), BF16), pltpu.SemaphoreType.DMA((3,))],
        compiler_params=pltpu.CompilerParams(vmem_limit_bytes=58 * 2**20),
        cost_estimate=pl.CostEstimate(
            flops=6 * SLOTS * D * D, bytes_accessed=6 * 2**20, transcendentals=0
        ),
    )(back, routed, hidden, logit, rows, grad, router, gain, wk, wv, wq)


def body(
    tokens,
    router,
    gain_one,
    bias_one,
    w_query,
    w_key,
    w_value,
    w_out,
    gain_two,
    bias_two,
    w_expand,
    w_contract,
    cotangent,
    seq_ids,
    routed_rows,
    routed_count,
):
    x_at = lax.axis_index("x").astype(jnp.int32)
    core_at = lax.axis_index("c").astype(jnp.int32)
    y_at = lax.axis_index(("yh", "yl")).astype(jnp.int32)
    z_at = lax.axis_index("z").astype(jnp.int32)
    first_at = jnp.where(core_at == 0, x_at, z_at)
    second_at = jnp.where(core_at == 0, z_at, x_at)
    row_index = routed_rows[0, 0]
    routed_total = routed_count[0, 0]
    x_local = tokens[0]
    place_at = lax.axis_index(("z", "c")).astype(jnp.int32)
    to_heads, normed_low, routed_x = embed(
        jnp.stack([routed_total, place_at]),
        routed_rows[0],
        seq_ids,
        x_local,
        gain_one,
        bias_one,
        w_key,
        w_value,
        w_query,
    )
    recv = swap(to_heads.reshape(64, SLOTS, 4 * HEAD), ("x",) + SIXTEEN)
    w_part = jnp.concatenate(
        [
            lax.dynamic_slice(
                w,
                (lax.axis_index(("x", "z", "yl")) * 24, (core_at * 2 + lax.axis_index("yh")) * 3 * HEAD),
                (24, 3 * HEAD),
            )
            for w in (w_key, w_value, w_query)
        ],
        axis=1,
    ).astype(F32)
    recv, w_part = lax.optimization_barrier((recv, w_part))
    recv = recv.reshape(4, 2, RUN, 4 * HEAD)
    normed_block = lax.all_gather(normed_low, SIXTEEN, axis=0, tiled=True)

    is_valid = jnp.arange(SLOTS, dtype=jnp.int32) < routed_total
    picks = row_index[:, None] == jnp.arange(TOK, dtype=jnp.int32)[None, :]
    pick_low = picks.astype(BF16)
    pick_full = picks.astype(F32)
    gate_value = jax.nn.sigmoid(jnp.sum(routed_x * router[None, :], axis=-1))
    gate_used = jnp.where(is_valid, gate_value, 0.0)
    grad_local = cotangent[0]
    grad_branch = gate_used[:, None] * mm(pick_low, grad_local)
    grad_contracted = grad_branch.astype(BF16)
    grad_activated = mm_nt(grad_contracted, w_contract)

    mixed_here, mixed_low, lse = attend(x_at[None], recv)
    mixed_parts = swap(mixed_low.reshape(16, SLOTS, 2 * HEAD), SIXTEEN)
    (kept, given, do_parts, projected, grad_hidden, grad_logit, vectors, activated_low) = feed(
        mixed_parts,
        routed_x,
        gate_value[:, None],
        grad_branch,
        grad_contracted,
        grad_activated,
        gain_two[None],
        bias_two[None],
        core_at[None],
        w_out,
        w_expand,
    )
    given = lax.ppermute(given, "c", [(0, 1), (1, 0)])
    eight = jnp.concatenate([kept, given], axis=1)
    eight = ring_swap(eight, first_at, lambda step: ring_pairs(0, step), CUBE_AXES)
    do_parts = swap(do_parts, SIXTEEN)
    eight, do_parts, normed_block = lax.optimization_barrier((eight, do_parts, normed_block))
    vectors = jnp.pad(vectors.astype(BF16).reshape(16, 48, 3), ((0, 0), (0, 0), (0, 29)))
    partial_grads = unit_grads(eight, vectors)
    do_parts, partial_grads = lax.optimization_barrier((do_parts, partial_grads))
    grad_q, grad_kv = attend_back(
        x_at[None], recv, do_parts.reshape(2, RUN, 2 * HEAD), mixed_here, lse
    )
    partial_grads = ring_swap(
        partial_grads, second_at, lambda step: ring_pairs(1, step), CUBE_AXES
    )
    partial_grads, grad_kv = lax.optimization_barrier((partial_grads, grad_kv))
    partial_grads = sum(part.astype(F32) for part in partial_grads).astype(BF16)
    partial_grads = ring_swap(
        partial_grads,
        y_at,
        lambda step: [(i, (i + step) % 4) for i in range(4)],
        ("yh", "yl"),
    )
    own_grads = sum(part.astype(F32) for part in partial_grads).astype(BF16)
    grad_kv, own_grads = lax.optimization_barrier((grad_kv, own_grads))
    grad_kv = swap(grad_kv, ("x",))
    grad_kv_sum = jnp.sum(grad_kv.astype(F32), axis=0).astype(BF16)
    grad_heads = jnp.concatenate(
        [grad_kv_sum.reshape(2 * RUN, 2 * HEAD), grad_q.reshape(2 * RUN, HEAD)], axis=1
    )
    units = lax.all_gather(own_grads, CHIPS, axis=0, tiled=False)
    branch = projected + mm(activated_low, w_contract)
    output = (
        x_local.astype(F32)
        + dot(pick_full, gate_used[:, None] * branch, ((0,), (0,)), EXACT)
    ).astype(BF16)

    grad_qkv = mm_tn(normed_block, grad_heads).astype(BF16).reshape(32, 24, 3 * HEAD)
    column_sum = jnp.sum(grad_heads.astype(F32), axis=0).astype(BF16).reshape(1, 3, HEAD)
    column_sum = jnp.broadcast_to(jnp.pad(column_sum, ((0, 0), (0, 21), (0, 0))), (32, 24, HEAD))
    grad_qkv = swap(jnp.concatenate([grad_qkv, column_sum], axis=2), ("x", "z", "yl"))
    grad_qkv, output = lax.optimization_barrier((grad_qkv, output))
    grad_qkv = jnp.sum(grad_qkv.reshape(4, 4, 2, 24, 4 * HEAD)[:, :3].astype(F32), axis=(0, 2))
    column_sum = grad_qkv[:, :3, 3 * HEAD :].transpose(1, 0, 2).reshape(9 * HEAD)
    grad_qkv = jnp.concatenate(
        [
            grad_qkv[:, :, kind * HEAD : (kind + 1) * HEAD].transpose(1, 0, 2).reshape(24, 3 * HEAD)
            for kind in range(3)
        ],
        axis=1,
    )
    norm_sums = jnp.stack(
        [jnp.sum(w_part * grad_qkv, axis=1), jnp.sum(w_part * column_sum[None, :], axis=1)], axis=1
    )
    own_qkv = jnp.concatenate([grad_qkv, jnp.pad(norm_sums, ((0, 0), (0, 62)))], axis=1)
    own_qkv = own_qkv.astype(BF16)
    heads = spread(own_qkv, CHIPS)
    heads, grad_heads = lax.optimization_barrier((heads, grad_heads))
    back = swap(
        jnp.pad(grad_heads, ((0, 0), (0, HEAD))).reshape(16, SLOTS, 4 * HEAD), SIXTEEN
    )
    heads_other = lax.ppermute(heads, "c", [(0, 1), (1, 0)])
    me = jnp.stack([x_at, y_at, z_at, core_at])
    final_key, final_value, final_query, norm_sums = place_heads(me, heads, heads_other)
    norm_sums = norm_sums[:, :2].T
    grad_gain_one = (norm_sums[0] - bias_one * norm_sums[1]) / gain_one
    grad_bias_one = norm_sums[1]
    units, back, final_key, grad_gain_one = lax.optimization_barrier(
        (units, back, final_key, grad_gain_one)
    )
    first = place(me, units)
    back, first = lax.optimization_barrier((back, first))
    input_grad = embed_back(
        back,
        routed_x,
        grad_hidden,
        grad_logit,
        routed_rows[0],
        grad_local,
        router,
        gain_one,
        w_key,
        w_value,
        w_query,
    )
    placed = place(me, other_core([units])[0], first)
    final_expand, final_contract, final_out = placed[:3]
    vectors = first[3] + placed[3]
    vectors = vectors[:, :, :3].reshape(3, D)
    return (
        output[None],
        input_grad[None],
        vectors[0],
        grad_gain_one,
        grad_bias_one,
        final_query,
        final_key,
        final_value,
        final_out,
        vectors[1],
        vectors[2],
        final_expand,
        final_contract,
    )


def solution(mesh):
    fine = Mesh(mesh.devices.reshape(2, 4, 4, 2, 2), ("yh", "x", "z", "c", "yl"))
    seq = ("yh", "x", "z", "c")
    in_specs = (
        (P("yl", seq, None),)
        + (P(),) * 11
        + (P("yl", seq, None), P("yl", seq), P("yl", seq, None), P("yl", seq))
    )
    out_specs = (P("yl", seq, None),) * 2 + (P(),) * 11
    return jax.shard_map(body, mesh=fine, in_specs=in_specs, out_specs=out_specs, check_vma=False)
```
